1024 devices in a mesh: tm: 64 (over z, y_hi, core), space: 16 (over y_lo, x).
Axes of the slice: x: 8, y: 8 (y_hi: 4, y_lo: 2; y = y_hi * 2 + y_lo), z: 8, core: 2. Of those that a mesh axis runs over, the one named last changes fastest.
Arguments:
- guess: float32 [64, 5, 64, 2048], P('tm', None, None, 'space'), may hold values from -6 to 6
- deriv: float32 [64, 64], replicated, may hold values from -0.75 to 0.75
- viscous: float32 [64, 64], replicated, may hold values from -0.75 to 0.75
- flux_jacobian: float32 [5, 5], replicated, may hold values from -2.5 to 2.5
- upwind: float32 [5, 5], replicated, may hold values from -2.5 to 2.5
- lift: float32 [64, 16], replicated, may hold values from -1.5 to 1.5
- restrict: float32 [8, 64], replicated, may hold values from -0.75 to 0.75
- prolong: float32 [64, 8], replicated, may hold values from -2 to 2
- coarse_self: float32 [40, 40], replicated
- coarse_group: float32 [40, 40], replicated
- neighbors: int32 [2048], P('space'), may hold values from 0 to 2047, as said below
- coarse_map: int32 [2048], replicated, may hold values from 0 to 2047, as said below
Outputs:
- starts: float32 [64, 5, 64, 2048], P('tm', None, None, 'space')
The draws below stay inside these ranges and needn't reach their ends.
Inputs may be any that keep to these rules, and one draw needn't show every extreme that they name: `neighbors`: the element across the upwind face of an element of partition p (elements p*128 to (p+1)*128 - 1) lies in partition p or in the partition before it, cyclically. `coarse_map`: a permutation of all elements; positions q*128 to (q+1)*128 - 1 take an equal share of elements from every partition, the shares in order of partition.
All inputs are finite; a program needn't handle non-finite values.
Results may differ from the reference program's by a relative error of at most 0.0003.
Values sent between devices are 32-bit elements; how exact they have to be, the bound alone decides.
A program may use at most 32 MiB of HBM per device.

```python
import math
import jax
import jax.numpy as jnp
from jax import lax

COMP = 5
NODES = 64
FACE = 16
CNODES = 8
GROUP = 4
SUB = 8
ITERS = 2
EL = 128
COARSE = 40
SLICES = 64
ELEMS = 2048
N_SPACE = 16


def draw_coarse_self(key, part):
    key = jax.random.fold_in(key, 21)
    noise = jax.random.uniform(key, (COARSE, COARSE), jnp.float32, -1.7320508, 1.7320508)
    return 0.84 * jnp.eye(COARSE, dtype=jnp.float32) + 0.14 / math.sqrt(COARSE) * noise


def draw_coarse_group(key, part):
    key = jax.random.fold_in(key, 22)
    noise = jax.random.uniform(key, (COARSE, COARSE), jnp.float32, -1.7320508, 1.7320508)
    return 0.08 / math.sqrt(COARSE) * noise


def draw_neighbors(key, part):
    key = jax.random.fold_in(key, 11)
    split_keys = jax.random.split(key, 2)
    orderings = jax.vmap(lambda subkey: jax.random.permutation(subkey, EL))(jax.random.split(split_keys[0], N_SPACE))
    orderings = orderings.astype(jnp.int32)
    upwind_side = jax.random.randint(split_keys[1], (N_SPACE, EL), 0, 2, dtype=jnp.int32)
    upwind_side = jnp.where((orderings == 0) | (orderings == EL - 1), 0, upwind_side)
    partition = jnp.arange(N_SPACE, dtype=jnp.int32)[:, None]
    return ((partition - upwind_side) % N_SPACE * EL + orderings).reshape(-1).astype(jnp.int32)


def draw_coarse_map(key, part):
    key = jax.random.fold_in(key, 31)
    orderings = jax.vmap(lambda subkey: jax.random.permutation(subkey, EL))(jax.random.split(key, N_SPACE))
    elements = orderings.astype(jnp.int32) + jnp.arange(N_SPACE, dtype=jnp.int32)[:, None] * EL
    grouped = elements.reshape(N_SPACE, N_SPACE, EL // N_SPACE)
    return jnp.transpose(grouped, (1, 0, 2)).reshape(-1).astype(jnp.int32)


def block_levels(own_key, shape, shards, least, high):
    loudness = 1.0
    for dim, blocks in shards:
        steps = jax.random.uniform(jax.random.fold_in(jax.random.fold_in(own_key, 6), dim), (blocks,), jnp.float32, least / len(shards), high / len(shards))
        loudness = loudness * jnp.repeat(jnp.exp(steps), shape[dim] // blocks).reshape((-1,) + (1,) * (len(shape) - 1 - dim))
    return loudness


def bell_draw(key, extent, width, bound, cuts=(), held_as=jnp.bfloat16):
    values = width * jax.random.normal(key, extent, jnp.float32)
    if cuts:
        values = values * block_levels(key, extent, cuts, -0.22, 0.18)
    return jnp.clip(values, -bound, bound).astype(held_as)


def setup_inputs(seed: int = 0) -> dict:
    arg_keys = jax.random.split(jax.random.key(seed), 13)
    guess = bell_draw(arg_keys[0], (SLICES, COMP, NODES, ELEMS), 1.0, 6.0, ((0, 64), (3, 16)), jnp.float32)
    deriv = bell_draw(arg_keys[1], (NODES, NODES), NODES ** -0.5, 0.75, (), jnp.float32)
    viscous = bell_draw(arg_keys[2], (NODES, NODES), NODES ** -0.5, 0.75, (), jnp.float32)
    flux_jacobian = bell_draw(arg_keys[3], (COMP, COMP), COMP ** -0.5, 2.5, (), jnp.float32)
    upwind = bell_draw(arg_keys[4], (COMP, COMP), COMP ** -0.5, 2.5, (), jnp.float32)
    lift = bell_draw(arg_keys[5], (NODES, FACE), FACE ** -0.5, 1.5, (), jnp.float32)
    restrict = bell_draw(arg_keys[6], (CNODES, NODES), NODES ** -0.5, 0.75, (), jnp.float32)
    prolong = bell_draw(arg_keys[7], (NODES, CNODES), CNODES ** -0.5, 2.0, (), jnp.float32)
    coarse_self = draw_coarse_self(jax.random.fold_in(arg_keys[12], 71), 0)
    coarse_group = draw_coarse_group(jax.random.fold_in(arg_keys[12], 71), 0)
    neighbors = draw_neighbors(jax.random.fold_in(arg_keys[12], 71), 0)
    coarse_map = draw_coarse_map(jax.random.fold_in(arg_keys[12], 71), 0)
    return dict(guess=guess, deriv=deriv, viscous=viscous, flux_jacobian=flux_jacobian, upwind=upwind, lift=lift, restrict=restrict, prolong=prolong, coarse_self=coarse_self, coarse_group=coarse_group, neighbors=neighbors, coarse_map=coarse_map)


highest = lax.Precision.HIGHEST
step_size = 0.08


def operator_terms(fields, upwind_traces, deriv, viscous, flux_jacobian, upwind, lift):
    derived = jnp.einsum("ij,cje->cie", deriv, fields, precision=highest)
    volume = jnp.einsum("ij,cje->cie", viscous, fields, precision=highest)
    volume = volume - jnp.einsum("cd,die->cie", flux_jacobian, derived, precision=highest)
    minus_trace = fields.reshape(COMP, FACE, 4, -1)[:, :, 0, :]
    face_jump = jnp.einsum("cd,dfe->cfe", upwind, upwind_traces - minus_trace, precision=highest)
    return volume + jnp.einsum("nf,cfe->cne", lift, face_jump, precision=highest)


def fine_sweep(fields, neighbors, deriv, viscous, flux_jacobian, upwind, lift):
    for substep in range(SUB):
        plus_trace = fields.reshape(COMP, FACE, 4, -1)[:, :, 3, :]
        upwind_traces = jnp.take(plus_trace, neighbors, axis=2)
        fields = fields + step_size * operator_terms(fields, upwind_traces, deriv, viscous, flux_jacobian, upwind, lift)
    return fields


def coarse_apply(self_matrix, group_matrix, values, span):
    grouped = values.reshape(values.shape[0], -1, GROUP, span)
    average = jnp.mean(grouped, axis=2)
    direct = jnp.einsum("ij,jpge->ipge", self_matrix, grouped, precision=highest)
    shared = jnp.einsum("ij,jpe->ipe", group_matrix, average, precision=highest)
    return (direct + shared[:, :, None, :]).reshape(values.shape)


def restrict_fields(restrict, fields):
    return jnp.einsum("mn,cne->cme", restrict, fields, precision=highest).reshape(COARSE, -1)


def prolong_fields(prolong, coarse_values):
    return jnp.einsum("nm,cme->cne", prolong, coarse_values.reshape(COMP, CNODES, -1), precision=highest)


def reference(guess, deriv, viscous, flux_jacobian, upwind, lift, restrict, prolong, coarse_self, coarse_group, neighbors, coarse_map):
    positions = jnp.zeros((ELEMS,), jnp.int32).at[coarse_map].set(jnp.arange(ELEMS, dtype=jnp.int32))
    starts = guess
    for sweep_number in range(ITERS):
        def propagate(fields):
            ends = fine_sweep(fields, neighbors, deriv, viscous, flux_jacobian, upwind, lift)
            coarse_pair = jnp.concatenate([restrict_fields(restrict, ends), restrict_fields(restrict, fields)], axis=0)
            return ends, jnp.take(coarse_pair, coarse_map, axis=1)

        ends, coarse_pairs = lax.map(propagate, starts)

        def advance(carry, coarse_pair):
            correction = coarse_apply(coarse_self, coarse_group, carry - coarse_pair[COARSE:], EL // GROUP)
            return correction + coarse_pair[:COARSE], correction

        last_state, corrections = lax.scan(advance, coarse_pairs[0, COARSE:], coarse_pairs)
        fine_corrections = jnp.take(corrections, positions, axis=2)
        candidates = ends + jax.vmap(lambda coarse_block: prolong_fields(prolong, coarse_block))(fine_corrections)
        starts = jnp.concatenate([starts[:1], candidates[:-1]], axis=0)
    return starts
```

```python
import functools

import jax
import jax.numpy as jnp
from jax import lax
from jax.experimental import pallas as pl
from jax.experimental.pallas import tpu as pltpu
from jax.sharding import PartitionSpec as P

COMP = 5
NODES = 64
FACE = 16
CNODES = 8
SUB = 8
ITERS = 2
COARSE = 40
EL = 128
WIDE = COMP * EL
NY = 4
NZ = 8
STEP = 0.08

f32 = jnp.float32
bf16 = jnp.bfloat16
highest = lax.Precision.HIGHEST
MESH = pl.DeviceIdType.MESH

HALO = 0
SEM_S = HALO + SUB * ITERS
SEM_F = SEM_S + ITERS
SEM_Y = SEM_F + 2 * ITERS
SEM_Z = SEM_Y + 3 * ITERS
SEM_P = SEM_Z + 7 * ITERS
SEM_Q = SEM_P + ITERS
SEM_END = SEM_Q + 3 * ITERS
SEMS = SEM_END + 1


def iota(shape, dim):
    return lax.broadcasted_iota(jnp.int32, shape, dim)


def dot(a, b):
    return jnp.dot(a, b, preferred_element_type=f32)


def dot32(a, b):
    return jnp.dot(a, b, precision=highest, preferred_element_type=f32)


def halves(x):
    high = x.astype(bf16)
    return high, (x - high.astype(f32)).astype(bf16)


def stack3(x):
    high, low = halves(x)
    return jnp.concatenate([high, high, low], axis=0)


def spread3(x, place):
    depth = x.shape[1]
    rows, cols = iota((depth, 3 * depth), 0), iota((depth, 3 * depth), 1)
    third = cols // depth
    hit = place(rows, cols - third * depth)
    high, low = halves(x)
    outer = jnp.where(hit & (third != 1), 1.0, 0.0).astype(bf16)
    middle = jnp.where(hit & (third == 1), 1.0, 0.0).astype(bf16)
    return (dot(high, outer) + dot(low, middle)).astype(bf16)


def same(row, col):
    return row == col


def node_place(row, col):
    return row == (col % FACE) * 4 + (col // FACE + 3) % 4


def node_rows(ref, start=0):
    return jnp.concatenate(
        [ref[pl.ds(start + i, FACE, stride=4), :] for i in (3, 0, 1, 2)], axis=0
    )


def part(x, c):
    return x[:, c * EL : (c + 1) * EL]


def pick(x, index):
    return jnp.take_along_axis(x, jnp.broadcast_to(index, x.shape), axis=1, mode="promise_in_bounds")


def tall(x):
    return jnp.concatenate([part(x, c) for c in range(COMP)], axis=0)


def wide(x):
    return jnp.concatenate([x[c * CNODES : (c + 1) * CNODES] for c in range(COMP)], axis=1)


def kernel(
    guess, deriv, viscous, jacobian, upwind, lift, restrict, prolong, self_ref, group_ref, neighbors, coarse_map,
    out,
    state, base, sent, landed, s_out, s_in, f_out, f_pair, t_all, z_out, z_all, p_pair, q_out, q_all, cand, fin,
    gen3, lift3, rst3, rl3, w_m, w_y, w_z, w_q, maps,
    ssem, rsem,
):
    tm, sp = lax.axis_index("tm"), lax.axis_index("space")
    core, chip = lax.rem(tm, 2), tm // 2
    yh, z = lax.rem(chip, NY), chip // NY
    slices, parts = 2 * NY * NZ, 16

    def at(t=None, s=None):
        return {"tm": tm if t is None else t, "space": sp if s is None else s}

    def chip_at(q, c):
        return at(2 * lax.rem(q + NY * NZ, NY * NZ) + c)

    def y_at(k):
        return at((z * NY + lax.rem(yh + k + NY, NY)) * 2 + core)

    def z_at(k):
        return at(lax.rem(tm + 2 * NY * k + slices, slices))

    def sp_at(k):
        return at(None, lax.rem(sp + k + parts, parts))

    sibling = at(tm + 1 - 2 * core)
    upper = at(lax.rem(tm + 1, slices))
    lower = at(lax.rem(tm + slices - 1, slices))

    def copy(src, dst, send, recv, to):
        return pltpu.make_async_remote_copy(
            src_ref=src, dst_ref=dst, send_sem=ssem.at[send], recv_sem=rsem.at[recv], device_id=to, device_id_type=MESH
        )

    def halo(n):
        return copy(sent.at[n], landed.at[n], HALO + n, HALO + n, sp_at(1))

    def s_copy(it):
        return copy(s_out.at[it], s_in.at[it], SEM_S + it, SEM_S + it, lower)

    def f_near():
        return copy(f_out.at[0], f_pair.at[0, core], SEM_F, SEM_F, sibling)

    def f_far(c):
        return copy(f_out.at[1], f_pair.at[1, core], SEM_F + 2 + c, SEM_F + 2 + core, chip_at(chip + 1, c))

    def y_copy(it, k):
        return copy(t_all.at[it, yh], t_all.at[it, yh], SEM_Y + 3 * it + k - 1, SEM_Y + 3 * it + k - 1, y_at(k))

    def z_copy(it, k):
        return copy(z_out.at[it], z_all.at[it, k - 1], SEM_Z + 7 * it + k - 1, SEM_Z + 7 * it + k - 1, z_at(k))

    def p_copy(it):
        return copy(p_pair.at[it, core], p_pair.at[it, core], SEM_P + it, SEM_P + it, sibling)

    def q_copy(it, k):
        return copy(q_out.at[it], q_all.at[it, k - 1], SEM_Q + 3 * it + k - 1, SEM_Q + 3 * it + k - 1, sp_at(4 * k))

    z_all[...] = jnp.zeros_like(z_all)
    f_pair[...] = jnp.zeros_like(f_pair)

    barrier = pltpu.get_barrier_semaphore()
    senders = [sp_at(-1), upper, sibling, chip_at(chip - 1, 0), chip_at(chip - 1, 1)]
    senders += [y_at(-k) for k in (1, 2, 3)] + [z_at(-k) for k in range(1, NZ)] + [sp_at(-4 * k) for k in (1, 2, 3)]
    for device in senders:
        pl.semaphore_signal(barrier, inc=1, device_id=device, device_id_type=MESH)

    for c in range(COMP):
        state[:, c * EL : (c + 1) * EL] = node_rows(guess, c * NODES)
    sent[0] = state[0:FACE, :]

    index = neighbors[...] % EL
    own = (neighbors[...] // EL) == jnp.broadcast_to(sp, (1, EL))
    own = jnp.broadcast_to(own, (FACE, EL))

    volume = jnp.concatenate([node_rows(viscous), node_rows(deriv)], axis=0) * STEP
    gen3[...] = spread3(volume, node_place)
    lift_rows = node_rows(lift) * STEP
    lift3[...] = spread3(lift_rows, same)

    pl.semaphore_wait(barrier, len(senders))
    halo(0).start()

    def substep(n, side):
        last = n % SUB == SUB - 1
        v = state[...]
        yz = dot(gen3[...], stack3(v))
        plus, minus = v[0:FACE], v[FACE : 2 * FACE]
        inner = [pick(part(plus, d), index) - part(minus, d) for d in range(COMP)]
        for c in range(COMP):
            total = part(v, c) + part(yz[0:NODES], c)
            for d in range(COMP):
                total = total - jacobian[c, d] * part(yz[NODES:], d)
            base[:, c * EL : (c + 1) * EL] = total
        if last:
            coarse_base = dot(rst3[...], stack3(base[...]))
        side()
        halo(n).wait_recv()
        jump = [jnp.where(own, inner[d], pick(landed[n, :, d * EL : (d + 1) * EL], index) - part(minus, d)) for d in range(COMP)]
        mixed = []
        for c in range(COMP):
            total = upwind[c, 0] * jump[0]
            for d in range(1, COMP):
                total = total + upwind[c, d] * jump[d]
            mixed.append(total)
        faces = stack3(jnp.concatenate(mixed, axis=1))
        if last:
            ends = coarse_base + dot(rl3[...], faces)
            state[...] = base[...] + dot(lift3[...], faces)
            return ends
        trace = base[0:FACE, :] + dot(lift3[0:FACE, :], faces)
        sent[n + 1] = trace
        halo(n + 1).start()
        state[0:FACE, :] = trace
        state[FACE:, :] = base[FACE:, :] + dot(lift3[FACE:, :], faces)

    def send_starts(it):
        s_out[it] = tall(dot(rst3[...], stack3(state[...])))
        s_copy(it).start()

    def restriction():
        full = restrict[...]
        rst3[...] = spread3(full, node_place)
        rows, cols = iota((NODES, NODES), 0), iota((NODES, NODES), 1)
        moved = dot32(full, jnp.where(node_place(rows, cols), 1.0, 0.0))
        rl3[...] = spread3(dot32(moved, lift_rows), same)
        send_starts(0)

    def orders():
        lane = iota((16, EL), 1)
        here = pick(coarse_map[...], sp * 8 + lane % 8)
        chosen = jnp.where(iota((16, EL), 0) == lane // 8, here.astype(f32), 0.0)
        member = jnp.sum(chosen, axis=0, keepdims=True) - jnp.broadcast_to(sp * EL, (1, EL)).astype(f32)
        grid = jnp.transpose(jnp.broadcast_to(member, (EL, EL)))
        hit = grid == iota((EL, EL), 1).astype(f32)
        back = jnp.sum(jnp.where(hit, iota((EL, EL), 0).astype(f32), 0.0), axis=0, keepdims=True)
        maps[0:8] = jnp.broadcast_to(member, (8, EL)).astype(jnp.int32)
        maps[8:16] = jnp.broadcast_to(back, (8, EL)).astype(jnp.int32)

    small = (COARSE, COARSE)
    second = jnp.broadcast_to(core, small) == 1
    eye = jnp.where(iota(small, 0) == iota(small, 1), 1.0, 0.0)
    zero = jnp.zeros(small, f32)

    def powers():
        m = self_ref[...] + jnp.where(second, group_ref[...], 0.0)
        w = dot32(m, m)
        w2 = dot32(w, w)
        w_m[0] = m
        w_m[1] = w
        w_m[2] = w2
        w_m[3] = dot32(w2, w)
        w_m[4] = dot32(w2, w2)

    def beside(blocks):
        count = len(blocks)
        total = None
        for k, block in enumerate(blocks):
            rows, cols = iota((COARSE, COARSE * count), 0), iota((COARSE, COARSE * count), 1)
            term = dot32(block, jnp.where(cols - COARSE * k == rows, 1.0, 0.0))
            total = term if total is None else total + term
        return total

    def by_yh(choices):
        place = jnp.broadcast_to(yh, small)
        value = choices[3]
        for j in (2, 1, 0):
            value = jnp.where(place == j, choices[j], value)
        return value

    def y_weights():
        w, w2, w3 = w_m[1], w_m[2], w_m[3]
        w_y[0:COARSE] = beside(
            [
                by_yh([zero, eye, w, w2]),
                by_yh([zero, zero, eye, w]),
                by_yh([zero, zero, zero, eye]),
                zero,
            ]
        )
        w_y[COARSE:] = beside([w3, w2, w, eye])

    def z_weights():
        w8 = w_m[4]
        weight = by_yh([eye, w_m[1], w_m[2], w_m[3]])
        weights = [weight]
        for k in range(NZ - 2):
            weight = dot32(weight, w8)
            weights.append(weight)
        w_z[...] = beside(weights)

    def q_weights():
        a, group = self_ref[...], group_ref[...]
        b = a + group
        a1 = jnp.where(second, dot32(a, a), a)
        b1 = jnp.where(second, dot32(b, b), b)
        w_q[0:COARSE] = beside([-0.25 * a1, 0.25 * b1, jnp.where(second, 0.25 * group, 0.0)])
        w_q[COARSE:] = beside([a1, zero, jnp.where(second, a, 0.0)])

    def chain(it, ends):
        s_copy(it).wait_recv()
        force = tall(ends) - s_in[it]
        f_out[it] = force
        if it == 0:
            f_near().start()
            f_pair[0, core] = force
            f_near().wait_recv()
        else:

            @pl.when(chip < NY * NZ - 1)
            def _():
                f_far(0).start()
                f_far(1).start()

            @pl.when(chip > 0)
            def _():
                for c in (0, 1):
                    copy(f_out.at[1], f_pair.at[1, c], SEM_F + 2, SEM_F + 2 + c, sibling).wait_recv()

        t_all[it, yh] = f_pair[it, 1] + dot32(w_m[0], f_pair[it, 0])
        for k in (2, 1, 3):
            y_copy(it, k).start()
        for k in (1, 2, 3):
            copy(z_out.at[it], t_all.at[it, lax.rem(yh + NY - k, NY)], SEM_Y, SEM_Y + 3 * it + k - 1, sibling).wait_recv()
        both = dot32(w_y[...], jnp.concatenate([t_all[it, j] for j in range(NY)], axis=0))
        z_out[it] = both[COARSE:]
        for k in (4, 3, 5, 2, 6, 1, 7):

            @pl.when(z + k < NZ)
            def _(k=k):
                z_copy(it, k).start()

        if it == 1:

            @pl.when(tm < slices - 2)
            def _():
                copy(state, fin, SEM_END, SEM_END, at(lax.rem(tm + 2, slices))).start()

        for k in range(1, NZ):

            @pl.when(z >= k)
            def _(k=k):
                z_copy(it, k).wait_recv()

        before = both[0:COARSE] + dot32(w_z[...], jnp.concatenate([z_all[it, k] for k in range(NZ - 1)], axis=0))
        p_pair[it, core] = before
        p_copy(it).start()
        copy(z_out.at[it], p_pair.at[it, 1 - core], SEM_P + it, SEM_P + it, sibling).wait_recv()
        both = dot32(w_q[...], jnp.concatenate([p_pair[it, 0], p_pair[it, 1], f_pair[it, 0]], axis=0))
        mine = pick(both[0:COARSE], maps[0:1])
        q_out[it] = mine
        for k in (3, 1, 2):
            q_copy(it, k).start()
        for k in (2, 1, 3):
            q_copy(it, k).wait_recv()
        mean = (mine + q_all[it, 0]) + (q_all[it, 1] + q_all[it, 2])
        return wide(both[COARSE:] + pick(mean, maps[8:9]))

    sides = [restriction, orders, powers, y_weights, z_weights, q_weights, lambda: None, lambda: None]
    for n in range(SUB):
        ends = substep(n, sides[n])
    correction = chain(0, ends)
    raise_by = node_rows(prolong)
    trace = state[0:FACE, :] + dot32(raise_by[0:FACE], correction)
    sent[SUB] = trace
    halo(SUB).start()
    state[0:FACE, :] = trace
    state[FACE:, :] = state[FACE:, :] + dot32(raise_by[FACE:], correction)

    first_to_second = copy(cand, fin, SEM_END, SEM_END, sibling)

    @pl.when(tm == 0)
    def _():
        cand[...] = state[...]
        first_to_second.start()
        for c in range(COMP):
            fin[:, c * EL : (c + 1) * EL] = node_rows(guess, c * NODES)

    for n in range(SUB, 2 * SUB):
        ends = substep(n, functools.partial(send_starts, 1) if n == SUB else lambda: None)
    correction = chain(1, ends)
    added = dot32(raise_by, correction)

    @pl.when(tm > 0)
    def _():
        first_to_second.wait_recv()

    for c in range(COMP):
        for k, i in enumerate((3, 0, 1, 2)):
            rows = slice(k * FACE, (k + 1) * FACE)
            out[pl.ds(c * NODES + i, FACE, stride=4), :] = fin[rows, c * EL : (c + 1) * EL] + part(added[rows], c)

    for n in range(2 * SUB):
        halo(n).wait_send()
    f_near().wait_send()
    for it in range(ITERS):
        s_copy(it).wait_send()
        for k in (1, 2, 3):
            y_copy(it, k).wait_send()
            q_copy(it, k).wait_send()
        p_copy(it).wait_send()
        for k in range(1, NZ):

            @pl.when(z + k < NZ)
            def _(k=k):
                z_copy(it, k).wait_send()

    @pl.when(chip < NY * NZ - 1)
    def _():
        f_far(0).wait_send()
        f_far(1).wait_send()

    @pl.when(tm == 0)
    def _():
        first_to_second.wait_send()

    @pl.when(tm < slices - 2)
    def _():
        copy(state, fin, SEM_END, SEM_END + 0, sibling).wait_send()


def body(guess, deriv, viscous, jacobian, upwind, lift, restrict, prolong, coarse_self, coarse_group, neighbors, coarse_map):
    vmem = pl.BlockSpec(memory_space=pltpu.VMEM)
    smem = pl.BlockSpec(memory_space=pltpu.SMEM)

    def buffer(*shape):
        return pltpu.VMEM(shape, f32)

    result = pl.pallas_call(
        kernel,
        out_shape=jax.ShapeDtypeStruct((COMP * NODES, EL), f32),
        in_specs=[vmem, vmem, vmem, smem, smem, vmem, vmem, vmem, vmem, vmem, vmem, vmem],
        out_specs=vmem,
        scratch_shapes=[
            buffer(NODES, WIDE),
            buffer(NODES, WIDE),
            buffer(2 * SUB, FACE, WIDE),
            buffer(2 * SUB, FACE, WIDE),
            buffer(ITERS, COARSE, EL),
            buffer(ITERS, COARSE, EL),
            buffer(ITERS, COARSE, EL),
            buffer(ITERS, 2, COARSE, EL),
            buffer(ITERS, NY, COARSE, EL),
            buffer(ITERS, COARSE, EL),
            buffer(ITERS, NZ - 1, COARSE, EL),
            buffer(ITERS, 2, COARSE, EL),
            buffer(ITERS, COARSE, EL),
            buffer(ITERS, 3, COARSE, EL),
            buffer(NODES, WIDE),
            buffer(NODES, WIDE),
            pltpu.VMEM((2 * NODES, 3 * NODES), bf16),
            pltpu.VMEM((NODES, 3 * FACE), bf16),
            pltpu.VMEM((CNODES, 3 * NODES), bf16),
            pltpu.VMEM((CNODES, 3 * FACE), bf16),
            buffer(5, COARSE, COARSE),
            buffer(2 * COARSE, NY * COARSE),
            buffer(COARSE, (NZ - 1) * COARSE),
            buffer(2 * COARSE, 3 * COARSE),
            pltpu.VMEM((16, EL), jnp.int32),
            pltpu.SemaphoreType.DMA((SEMS,)),
            pltpu.SemaphoreType.DMA((SEMS,)),
        ],
        compiler_params=pltpu.CompilerParams(
            collective_id=0, has_side_effects=True, vmem_limit_bytes=32 * 2**20
        ),
        name="parareal",
    )(
        guess.reshape(COMP * NODES, EL), deriv, viscous, jacobian, upwind, lift, restrict, prolong,
        coarse_self, coarse_group, neighbors.reshape(1, EL), coarse_map.reshape(16, EL),
    )
    return result.reshape(1, COMP, NODES, EL)


def solution(mesh):
    return jax.shard_map(
        body,
        mesh=mesh,
        in_specs=(
            P("tm", None, None, "space"),
            P(), P(), P(), P(), P(), P(), P(), P(), P(),
            P("space"),
            P(),
        ),
        out_specs=P("tm", None, None, "space"),
        check_vma=False,
    )
```

```python
import functools

import jax
import jax.numpy as jnp
from jax import lax
from jax.experimental import pallas as pl
from jax.experimental.pallas import tpu as pltpu
from jax.sharding import PartitionSpec as P

COMP = 5
NODES = 64
FACE = 16
CNODES = 8
SUB = 8
ITERS = 2
COARSE = 40
EL = 128
WIDE = COMP * EL
NY = 4
NZ = 8
STEP = 0.08

f32 = jnp.float32
bf16 = jnp.bfloat16
highest = lax.Precision.HIGHEST
MESH = pl.DeviceIdType.MESH

PAIRS = SUB // 2
TRACE = 0
TRACE2 = TRACE + PAIRS * ITERS
AHEAD = TRACE2 + PAIRS * ITERS
SEM_NB = AHEAD + PAIRS * ITERS
SEM_S = SEM_NB + 1
SEM_F = SEM_S + ITERS
SEM_Y = SEM_F + 2 * ITERS
SEM_Z = SEM_Y + 3 * ITERS
SEM_P = SEM_Z + 7 * ITERS
SEM_Q = SEM_P + ITERS
SEM_END = SEM_Q + 3 * ITERS
SEMS = SEM_END + 1
INPUTS = 12


def iota(shape, dim):
    return lax.broadcasted_iota(jnp.int32, shape, dim)


def dot(a, b):
    return jnp.dot(a, b, preferred_element_type=f32)


def dot32(a, b):
    return jnp.dot(a, b, precision=highest, preferred_element_type=f32)


def halves(x):
    high = x.astype(bf16)
    return high, (x - high.astype(f32)).astype(bf16)


def stack3(x):
    high, low = halves(x)
    return jnp.concatenate([high, high, low], axis=0)


def spread3(x, place):
    depth = x.shape[1]
    rows, cols = iota((depth, 3 * depth), 0), iota((depth, 3 * depth), 1)
    third = cols // depth
    hit = place(rows, cols - third * depth)
    high, low = halves(x)
    outer = jnp.where(hit & (third != 1), 1.0, 0.0).astype(bf16)
    middle = jnp.where(hit & (third == 1), 1.0, 0.0).astype(bf16)
    return (dot(high, outer) + dot(low, middle)).astype(bf16)


def same(row, col):
    return row == col


def node_place(row, col):
    return row == (col % FACE) * 4 + (col // FACE + 3) % 4


def node_rows(ref, start=0):
    return jnp.concatenate(
        [ref[pl.ds(start + i, FACE, stride=4), :] for i in (3, 0, 1, 2)], axis=0
    )


def part(x, c):
    return x[:, c * EL : (c + 1) * EL]


def pick(x, index):
    return jnp.take_along_axis(x, jnp.broadcast_to(index, x.shape), axis=1, mode="promise_in_bounds")


def tall(x):
    return jnp.concatenate([part(x, c) for c in range(COMP)], axis=0)


def wide(x):
    return jnp.concatenate([x[c * CNODES : (c + 1) * CNODES] for c in range(COMP)], axis=1)


def kernel(
    guess_in, deriv_in, viscous_in, jacobian_in, upwind_in, lift_in, restrict_in, prolong_in, self_in, group_in,
    neighbors_in, coarse_map_in,
    out,
    guess, deriv, viscous, jacobian, upwind, lift, restrict, prolong, self_ref, group_ref, neighbors, coarse_map,
    state, base, trace_out, ahead_out, trace_in, trace2_in, ahead_in, nb_out, nb_in, s_out, s_in, f_out, f_pair, t_all, z_out, z_all, p_pair, q_out, q_all, cand, fin,
    gen3, lift3, rst3, rl3, w_m, w_y, w_z, w_q, maps,
    ssem, rsem, isem, ready,
):
    loads = [
        pltpu.make_async_copy(src, dst, isem.at[k])
        for k, (src, dst) in enumerate(
            [
                (guess_in, guess),
                (viscous_in, viscous),
                (deriv_in, deriv),
                (lift_in, lift),
                (neighbors_in, neighbors),
                (jacobian_in, jacobian),
                (upwind_in, upwind),
                (restrict_in, restrict),
                (self_in, self_ref),
                (group_in, group_ref),
                (coarse_map_in, coarse_map),
                (prolong_in, prolong),
            ]
        )
    ]
    for load in loads:
        load.start()
    tm, sp = lax.axis_index("tm"), lax.axis_index("space")
    core, chip = lax.rem(tm, 2), tm // 2
    yh, z = lax.rem(chip, NY), chip // NY
    slices, parts = 2 * NY * NZ, 16

    def at(t=None, s=None):
        return {"tm": tm if t is None else t, "space": sp if s is None else s}

    def chip_at(q, c):
        return at(2 * lax.rem(q + NY * NZ, NY * NZ) + c)

    def y_at(k):
        return at((z * NY + lax.rem(yh + k + NY, NY)) * 2 + core)

    def z_at(k):
        return at(lax.rem(tm + 2 * NY * k + slices, slices))

    def sp_at(k):
        return at(None, lax.rem(sp + k + parts, parts))

    sibling = at(tm + 1 - 2 * core)
    upper = at(lax.rem(tm + 1, slices))
    lower = at(lax.rem(tm + slices - 1, slices))

    def copy(src, dst, send, recv, to):
        return pltpu.make_async_remote_copy(
            src_ref=src, dst_ref=dst, send_sem=ssem.at[send], recv_sem=rsem.at[recv], device_id=to, device_id_type=MESH
        )

    def trace_copy(n):
        return copy(trace_out.at[n], trace_in.at[n], TRACE + n, TRACE + n, sp_at(1))

    def trace2_copy(n):
        return copy(trace_out.at[n], trace2_in.at[n], TRACE2 + n, TRACE2 + n, sp_at(2))

    def ahead_copy(n):
        return copy(ahead_out.at[n], ahead_in.at[n], AHEAD + n, AHEAD + n, sp_at(1))

    def nb_copy():
        return copy(nb_out, nb_in, SEM_NB, SEM_NB, sp_at(1))

    def send_trace(n, trace):
        trace_out[n] = trace
        trace2_copy(n).start()
        trace_copy(n).start()

    def s_copy(it):
        return copy(s_out.at[it], s_in.at[it], SEM_S + it, SEM_S + it, lower)

    def f_near():
        return copy(f_out.at[0], f_pair.at[0, core], SEM_F, SEM_F, sibling)

    def f_far(c):
        return copy(f_out.at[1], f_pair.at[1, core], SEM_F + 2 + c, SEM_F + 2 + core, chip_at(chip + 1, c))

    def y_copy(it, k):
        return copy(t_all.at[it, yh], t_all.at[it, yh], SEM_Y + 3 * it + k - 1, SEM_Y + 3 * it + k - 1, y_at(k))

    def z_copy(it, k):
        return copy(z_out.at[it], z_all.at[it, k - 1], SEM_Z + 7 * it + k - 1, SEM_Z + 7 * it + k - 1, z_at(k))

    def p_copy(it):
        return copy(p_pair.at[it, core], p_pair.at[it, core], SEM_P + it, SEM_P + it, sibling)

    def q_copy(it, k):
        return copy(q_out.at[it], q_all.at[it, k - 1], SEM_Q + 3 * it + k - 1, SEM_Q + 3 * it + k - 1, sp_at(4 * k))

    z_all[...] = jnp.zeros_like(z_all)
    f_pair[...] = jnp.zeros_like(f_pair)
    s_in[...] = jnp.zeros_like(s_in)

    chips = NY * NZ
    barrier = pltpu.get_barrier_semaphore()

    def tell(semaphore, device):
        pl.semaphore_signal(semaphore, inc=1, device_id=device, device_id_type=MESH)

    for device in [sp_at(-1), sp_at(-2), sp_at(4), sp_at(8), sp_at(12), sibling]:
        tell(barrier, device)

    @pl.when(tm < slices - 1)
    def _():
        tell(barrier, upper)

    @pl.when(chip < chips - 1)
    def _():
        tell(barrier, chip_at(chip + 1, 0))
        tell(barrier, chip_at(chip + 1, 1))

    for k in range(1, NY):

        @pl.when(yh + k < NY)
        def _(k=k):
            tell(barrier, y_at(k))

    for k in range(1, NZ):

        @pl.when(z + k < NZ)
        def _(k=k):
            tell(barrier, z_at(k))

    heard = 6 + lax.min(tm, 1) + 2 * lax.min(chip, 1) + yh + z

    def report():
        @pl.when(chip > 0)
        def _():
            tell(ready.at[2], chip_at(chip - 1, 0))
            tell(ready.at[2], chip_at(chip - 1, 1))

        for k in range(1, NY):

            @pl.when(yh - k >= 0)
            def _(k=k):
                tell(ready.at[0], y_at(-k))

        for k in range(1, NZ):

            @pl.when(z - k >= 0)
            def _(k=k):
                tell(ready.at[1], z_at(-k))

    def hear(which, count):
        @pl.when(count > 0)
        def _():
            pl.semaphore_wait(ready.at[which], count)

    rows, cols = iota((NODES, NODES), 0), iota((NODES, NODES), 1)
    reorder = jnp.where(node_place(cols, rows), 1.0, 0.0)

    def reordered(flipped):
        return lax.dot_general(
            reorder, flipped, (((1,), (1,)), ((), ())), precision=highest, preferred_element_type=f32
        )

    loads[0].wait()
    for c in range(COMP):
        state[:, c * EL : (c + 1) * EL] = node_rows(guess, c * NODES)
    for load in loads[1:7]:
        load.wait()

    def sides(numbers, place):
        here = (numbers // EL) == jnp.broadcast_to(place, (1, EL))
        return numbers % EL, jnp.broadcast_to(here, (FACE, EL))

    index, own = sides(neighbors[...], sp)
    nb_out[...] = jnp.broadcast_to(neighbors[...].astype(f32), (8, EL))

    pl.semaphore_wait(barrier, heard)
    send_trace(0, state[0:FACE, :])
    nb_copy().start()
    report()

    volume = jnp.concatenate([node_rows(viscous), node_rows(deriv)], axis=0) * STEP
    gen3[...] = spread3(volume, node_place)
    lift_rows = reordered(lift[...]) * STEP
    lift3[...] = spread3(lift_rows, same)

    def volume_part(v, dest):
        yz = dot(gen3[...], stack3(v))
        for c in range(COMP):
            total = part(v, c) + part(yz[0:NODES], c)
            for d in range(COMP):
                total = total - jacobian[c, d] * part(yz[NODES:], d)
            dest[:, c * EL : (c + 1) * EL] = total

    def faces(jump):
        mixed = []
        for c in range(COMP):
            total = upwind[c, 0] * jump[0]
            for d in range(1, COMP):
                total = total + upwind[c, d] * jump[d]
            mixed.append(total)
        return stack3(jnp.concatenate(mixed, axis=1))

    def pair(n, side):
        last = n % PAIRS == PAIRS - 1
        v = state[...]
        volume_part(v, base)
        minus = [part(v[FACE : 2 * FACE], d) for d in range(COMP)]
        inner = [pick(part(v[0:FACE], d), index) for d in range(COMP)]
        known = faces([jnp.where(own, inner[d], 0.0) - minus[d] for d in range(COMP)])
        ahead_out[n] = base[0:FACE, :] + dot(lift3[0:FACE, :], known)
        ahead_copy(n).start()
        side()
        if n == 0:
            nb_copy().wait_recv()
        trace_copy(n).wait_recv()
        jump = [
            jnp.where(own, inner[d], pick(trace_in[n, :, d * EL : (d + 1) * EL], index)) - minus[d] for d in range(COMP)
        ]
        v = base[...] + dot(lift3[...], faces(jump))
        volume_part(v, base)
        if last:
            coarse_base = dot(rst3[...], stack3(base[...]))
        minus = [part(v[FACE : 2 * FACE], d) for d in range(COMP)]
        inner = [pick(part(v[0:FACE], d), index) for d in range(COMP)]
        index_before, own_before = sides(nb_in[0:1, :].astype(jnp.int32), lax.rem(sp + parts - 1, parts))
        trace2_copy(n).wait_recv()
        jump = [
            jnp.where(own_before, 0.0, pick(trace2_in[n, :, d * EL : (d + 1) * EL], index_before)) for d in range(COMP)
        ]
        missing = dot(lift3[0:FACE, :], faces(jump))
        ahead_copy(n).wait_recv()
        before = ahead_in[n] + missing
        jump = [jnp.where(own, inner[d], pick(part(before, d), index)) - minus[d] for d in range(COMP)]
        entering = faces(jump)
        if last:
            ends = coarse_base + dot(rl3[...], entering)
            state[...] = base[...] + dot(lift3[...], entering)
            return ends
        trace = base[0:FACE, :] + dot(lift3[0:FACE, :], entering)
        send_trace(n + 1, trace)
        state[0:FACE, :] = trace
        state[FACE:, :] = base[FACE:, :] + dot(lift3[FACE:, :], entering)

    def send_starts(it):
        s_out[it] = tall(dot(rst3[...], stack3(state[...])))

        @pl.when(tm > 0)
        def _():
            s_copy(it).start()

    def restriction():
        for load in loads[7:]:
            load.wait()
        full = restrict[...]
        rst3[...] = spread3(full, node_place)
        moved = dot32(full, jnp.where(node_place(rows, cols), 1.0, 0.0))
        rl3[...] = spread3(dot32(moved, lift_rows), same)
        send_starts(0)

    def orders():
        lane = iota((16, EL), 1)
        here = pick(coarse_map[...], sp * 8 + lane % 8)
        chosen = jnp.where(iota((16, EL), 0) == lane // 8, here.astype(f32), 0.0)
        member = jnp.sum(chosen, axis=0, keepdims=True) - jnp.broadcast_to(sp * EL, (1, EL)).astype(f32)
        grid = jnp.transpose(jnp.broadcast_to(member, (EL, EL)))
        hit = grid == iota((EL, EL), 1).astype(f32)
        back = jnp.sum(jnp.where(hit, iota((EL, EL), 0).astype(f32), 0.0), axis=0, keepdims=True)
        maps[0:8] = jnp.broadcast_to(member, (8, EL)).astype(jnp.int32)
        maps[8:16] = jnp.broadcast_to(back, (8, EL)).astype(jnp.int32)

    small = (COARSE, COARSE)
    second = jnp.broadcast_to(core, small) == 1
    eye = jnp.where(iota(small, 0) == iota(small, 1), 1.0, 0.0)
    zero = jnp.zeros(small, f32)

    def powers():
        m = self_ref[...] + jnp.where(second, group_ref[...], 0.0)
        w = dot32(m, m)
        w2 = dot32(w, w)
        w_m[0] = m
        w_m[1] = w
        w_m[2] = w2
        w_m[3] = dot32(w2, w)
        w_m[4] = dot32(w2, w2)

    def beside(blocks):
        count = len(blocks)
        total = None
        for k, block in enumerate(blocks):
            rows, cols = iota((COARSE, COARSE * count), 0), iota((COARSE, COARSE * count), 1)
            term = dot32(block, jnp.where(cols - COARSE * k == rows, 1.0, 0.0))
            total = term if total is None else total + term
        return total

    def by_yh(choices):
        place = jnp.broadcast_to(yh, small)
        value = choices[3]
        for j in (2, 1, 0):
            value = jnp.where(place == j, choices[j], value)
        return value

    def y_weights():
        w, w2, w3 = w_m[1], w_m[2], w_m[3]
        w_y[0:COARSE] = beside(
            [
                by_yh([zero, eye, w, w2]),
                by_yh([zero, zero, eye, w]),
                by_yh([zero, zero, zero, eye]),
                zero,
            ]
        )
        w_y[COARSE:] = beside([w3, w2, w, eye])

    def z_weights():
        w8 = w_m[4]
        weight = by_yh([eye, w_m[1], w_m[2], w_m[3]])
        weights = [weight]
        for k in range(NZ - 2):
            weight = dot32(weight, w8)
            weights.append(weight)
        w_z[...] = beside(weights)

    def q_weights():
        a, group = self_ref[...], group_ref[...]
        b = a + group
        a1 = jnp.where(second, dot32(a, a), a)
        b1 = jnp.where(second, dot32(b, b), b)
        w_q[0:COARSE] = beside([-0.25 * a1, 0.25 * b1, jnp.where(second, 0.25 * group, 0.0)])
        w_q[COARSE:] = beside([a1, zero, jnp.where(second, a, 0.0)])

    def chain(it, ends):
        @pl.when(tm < slices - 1)
        def _():
            s_copy(it).wait_recv()

        force = tall(ends) - s_in[it]
        f_out[it] = force
        if it == 0:
            f_near().start()
            f_pair[0, core] = force
            f_near().wait_recv()
        else:
            hear(2, 2 * lax.min(chips - 1 - chip, 1))

            @pl.when(chip < chips - 1)
            def _():
                f_far(0).start()
                f_far(1).start()

            @pl.when(chip > 0)
            def _():
                for c in (0, 1):
                    copy(f_out.at[1], f_pair.at[1, c], SEM_F + 2, SEM_F + 2 + c, sibling).wait_recv()

        t_all[it, yh] = f_pair[it, 1] + dot32(w_m[0], f_pair[it, 0])
        if it == 0:
            hear(0, NY - 1 - yh)
        for k in (2, 1, 3):
            y_copy(it, k).start()
        for k in (1, 2, 3):
            copy(z_out.at[it], t_all.at[it, lax.rem(yh + NY - k, NY)], SEM_Y, SEM_Y + 3 * it + k - 1, sibling).wait_recv()
        both = dot32(w_y[...], jnp.concatenate([t_all[it, j] for j in range(NY)], axis=0))
        z_out[it] = both[COARSE:]
        if it == 0:
            hear(1, NZ - 1 - z)
        for k in (4, 3, 5, 2, 6, 1, 7):

            @pl.when(z + k < NZ)
            def _(k=k):
                z_copy(it, k).start()

        if it == 1:

            @pl.when(tm < slices - 2)
            def _():
                copy(state, fin, SEM_END, SEM_END, at(lax.rem(tm + 2, slices))).start()

        for k in range(1, NZ):

            @pl.when(z >= k)
            def _(k=k):
                z_copy(it, k).wait_recv()

        before = both[0:COARSE] + dot32(w_z[...], jnp.concatenate([z_all[it, k] for k in range(NZ - 1)], axis=0))
        p_pair[it, core] = before
        p_copy(it).start()
        copy(z_out.at[it], p_pair.at[it, 1 - core], SEM_P + it, SEM_P + it, sibling).wait_recv()
        both = dot32(w_q[...], jnp.concatenate([p_pair[it, 0], p_pair[it, 1], f_pair[it, 0]], axis=0))
        mine = pick(both[0:COARSE], maps[0:1])
        q_out[it] = mine
        for k in (3, 1, 2):
            q_copy(it, k).start()
        for k in (2, 1, 3):
            q_copy(it, k).wait_recv()
        mean = (mine + q_all[it, 0]) + (q_all[it, 1] + q_all[it, 2])
        return wide(both[COARSE:] + pick(mean, maps[8:9]))

    def after(*steps):
        for step in steps:
            step()

    tasks = [
        functools.partial(after, restriction, orders),
        functools.partial(after, powers, y_weights),
        functools.partial(after, z_weights),
        functools.partial(after, q_weights),
    ]
    for n in range(PAIRS):
        ends = pair(n, tasks[n])
    correction = chain(0, ends)
    raise_by = reordered(prolong[...])
    trace = state[0:FACE, :] + dot32(raise_by[0:FACE], correction)
    send_trace(PAIRS, trace)
    state[0:FACE, :] = trace
    state[FACE:, :] = state[FACE:, :] + dot32(raise_by[FACE:], correction)

    first_to_second = copy(cand, fin, SEM_END, SEM_END, sibling)

    @pl.when(tm == 0)
    def _():
        cand[...] = state[...]
        first_to_second.start()
        for c in range(COMP):
            fin[:, c * EL : (c + 1) * EL] = node_rows(guess, c * NODES)

    for n in range(PAIRS, 2 * PAIRS):
        ends = pair(n, functools.partial(send_starts, 1) if n == PAIRS else after)
    correction = chain(1, ends)
    added = dot32(raise_by, correction)

    @pl.when(tm > 0)
    def _():
        first_to_second.wait_recv()

    for c in range(COMP):
        for k, i in enumerate((3, 0, 1, 2)):
            rows = slice(k * FACE, (k + 1) * FACE)
            out[pl.ds(c * NODES + i, FACE, stride=4), :] = fin[rows, c * EL : (c + 1) * EL] + part(added[rows], c)

    nb_copy().wait_send()
    for n in range(2 * PAIRS):
        trace_copy(n).wait_send()
        trace2_copy(n).wait_send()
        ahead_copy(n).wait_send()
    f_near().wait_send()
    for it in range(ITERS):

        @pl.when(tm > 0)
        def _(it=it):
            s_copy(it).wait_send()

        for k in (1, 2, 3):
            y_copy(it, k).wait_send()
            q_copy(it, k).wait_send()
        p_copy(it).wait_send()
        for k in range(1, NZ):

            @pl.when(z + k < NZ)
            def _(k=k):
                z_copy(it, k).wait_send()

    @pl.when(chip < chips - 1)
    def _():
        f_far(0).wait_send()
        f_far(1).wait_send()

    @pl.when(tm == 0)
    def _():
        first_to_second.wait_send()

    @pl.when(tm < slices - 2)
    def _():
        copy(state, fin, SEM_END, SEM_END + 0, sibling).wait_send()


def body(guess, deriv, viscous, jacobian, upwind, lift, restrict, prolong, coarse_self, coarse_group, neighbors, coarse_map):
    hbm = pl.BlockSpec(memory_space=pltpu.HBM)

    def buffer(*shape):
        return pltpu.VMEM(shape, f32)

    result = pl.pallas_call(
        kernel,
        out_shape=jax.ShapeDtypeStruct((COMP * NODES, EL), f32),
        in_specs=[hbm] * INPUTS,
        out_specs=pl.BlockSpec(memory_space=pltpu.VMEM),
        scratch_shapes=[
            buffer(COMP * NODES, EL),
            buffer(NODES, NODES),
            buffer(NODES, NODES),
            pltpu.SMEM((COMP, COMP), f32),
            pltpu.SMEM((COMP, COMP), f32),
            buffer(FACE, NODES),
            buffer(CNODES, NODES),
            buffer(CNODES, NODES),
            buffer(COARSE, COARSE),
            buffer(COARSE, COARSE),
            pltpu.VMEM((1, EL), jnp.int32),
            pltpu.VMEM((16, EL), jnp.int32),
            buffer(NODES, WIDE),
            buffer(NODES, WIDE),
            buffer(2 * PAIRS, FACE, WIDE),
            buffer(2 * PAIRS, FACE, WIDE),
            buffer(2 * PAIRS, FACE, WIDE),
            buffer(2 * PAIRS, FACE, WIDE),
            buffer(2 * PAIRS, FACE, WIDE),
            buffer(8, EL),
            buffer(8, EL),
            buffer(ITERS, COARSE, EL),
            buffer(ITERS, COARSE, EL),
            buffer(ITERS, COARSE, EL),
            buffer(ITERS, 2, COARSE, EL),
            buffer(ITERS, NY, COARSE, EL),
            buffer(ITERS, COARSE, EL),
            buffer(ITERS, NZ - 1, COARSE, EL),
            buffer(ITERS, 2, COARSE, EL),
            buffer(ITERS, COARSE, EL),
            buffer(ITERS, 3, COARSE, EL),
            buffer(NODES, WIDE),
            buffer(NODES, WIDE),
            pltpu.VMEM((2 * NODES, 3 * NODES), bf16),
            pltpu.VMEM((NODES, 3 * FACE), bf16),
            pltpu.VMEM((CNODES, 3 * NODES), bf16),
            pltpu.VMEM((CNODES, 3 * FACE), bf16),
            buffer(5, COARSE, COARSE),
            buffer(2 * COARSE, NY * COARSE),
            buffer(COARSE, (NZ - 1) * COARSE),
            buffer(2 * COARSE, 3 * COARSE),
            pltpu.VMEM((16, EL), jnp.int32),
            pltpu.SemaphoreType.DMA((SEMS,)),
            pltpu.SemaphoreType.DMA((SEMS,)),
            pltpu.SemaphoreType.DMA((INPUTS,)),
            pltpu.SemaphoreType.REGULAR((3,)),
        ],
        compiler_params=pltpu.CompilerParams(
            collective_id=0, has_side_effects=True, vmem_limit_bytes=60 * 2**20
        ),
        name="parareal",
    )(
        guess.reshape(COMP * NODES, EL), deriv, viscous, jacobian, upwind, lift.T, restrict, prolong.T,
        coarse_self, coarse_group, neighbors.reshape(1, EL), coarse_map.reshape(16, EL),
    )
    return result.reshape(1, COMP, NODES, EL)


def solution(mesh):
    return jax.shard_map(
        body,
        mesh=mesh,
        in_specs=(
            P("tm", None, None, "space"),
            P(), P(), P(), P(), P(), P(), P(), P(), P(),
            P("space"),
            P(),
        ),
        out_specs=P("tm", None, None, "space"),
        check_vma=False,
    )
```

```python
import functools

import jax
import jax.numpy as jnp
from jax import lax
from jax.experimental import pallas as pl
from jax.experimental.pallas import tpu as pltpu
from jax.sharding import PartitionSpec as P

COMP = 5
NODES = 64
FACE = 16
CNODES = 8
SUB = 8
ITERS = 2
COARSE = 40
EL = 128
WIDE = COMP * EL
NY = 4
NZ = 8
STEP = 0.08

f32 = jnp.float32
bf16 = jnp.bfloat16
highest = lax.Precision.HIGHEST
MESH = pl.DeviceIdType.MESH

PAIRS = SUB // 2
TRACE = 0
TRACE2 = TRACE + PAIRS * ITERS
AHEAD = TRACE2 + PAIRS * ITERS
SEM_NB = AHEAD + PAIRS * ITERS
SEM_S = SEM_NB + 1
SEM_F = SEM_S + ITERS
SEM_LATE = SEM_F + ITERS
SEM_Y = SEM_LATE + 1
SEM_Z = SEM_Y + NY * ITERS
SEM_PRE = SEM_Z + (NZ - 1) * ITERS
SEM_P = SEM_PRE + ITERS
SEM_Q = SEM_P + ITERS
SEM_END = SEM_Q + 3 * ITERS
SEMS = SEM_END + 1
INPUTS = 12


def iota(shape, dim):
    return lax.broadcasted_iota(jnp.int32, shape, dim)


def dot(a, b):
    return jnp.dot(a, b, preferred_element_type=f32)


def dot32(a, b):
    return jnp.dot(a, b, precision=highest, preferred_element_type=f32)


def dot3(weights, x):
    high, low = halves(x)
    return dot(weights[0], high) + (dot(weights[1], high) + dot(weights[0], low))


def halves(x):
    high = x.astype(bf16)
    return high, (x - high.astype(f32)).astype(bf16)


def stack3(x):
    high, low = halves(x)
    return jnp.concatenate([high, high, low], axis=0)


def spread3(x, place):
    depth = x.shape[1]
    rows, cols = iota((depth, 3 * depth), 0), iota((depth, 3 * depth), 1)
    third = cols // depth
    hit = place(rows, cols - third * depth)
    high, low = halves(x)
    outer = jnp.where(hit & (third != 1), 1.0, 0.0).astype(bf16)
    middle = jnp.where(hit & (third == 1), 1.0, 0.0).astype(bf16)
    return (dot(high, outer) + dot(low, middle)).astype(bf16)


def same(row, col):
    return row == col


def node_place(row, col):
    return row == (col % FACE) * 4 + (col // FACE + 3) % 4


def node_rows(ref, start=0):
    return jnp.concatenate(
        [ref[pl.ds(start + i, FACE, stride=4), :] for i in (3, 0, 1, 2)], axis=0
    )


def part(x, c):
    return x[:, c * EL : (c + 1) * EL]


def pick(x, index):
    return jnp.take_along_axis(x, jnp.broadcast_to(index, x.shape), axis=1, mode="promise_in_bounds")


def tall(x):
    return jnp.concatenate([part(x, c) for c in range(COMP)], axis=0)


def wide(x):
    return jnp.concatenate([x[c * CNODES : (c + 1) * CNODES] for c in range(COMP)], axis=1)


def kernel(
    guess_in, deriv_in, viscous_in, jacobian_in, upwind_in, lift_in, restrict_in, prolong_in, self_in, group_in,
    neighbors_in, coarse_map_in,
    out,
    guess, deriv, viscous, jacobian, upwind, lift, restrict, prolong, self_ref, group_ref, neighbors, coarse_map,
    state, base, trace_out, ahead_out, trace_in, trace2_in, ahead_in, nb_out, nb_in, s_out, s_in, f_out, f_pair, f_late, t_out, t_all, z_out, z_all, pre, late, q_out, q_all, cand, fin,
    gen3, lift3, rst3, rl3, w_m, w_t, w_y, w_z, w_q, maps,
    ssem, rsem, isem, ready,
):
    loads = [
        pltpu.make_async_copy(src, dst, isem.at[k])
        for k, (src, dst) in enumerate(
            [
                (guess_in, guess),
                (viscous_in, viscous),
                (deriv_in, deriv),
                (lift_in, lift),
                (neighbors_in, neighbors),
                (jacobian_in, jacobian),
                (upwind_in, upwind),
                (restrict_in, restrict),
                (self_in, self_ref),
                (group_in, group_ref),
                (coarse_map_in, coarse_map),
                (prolong_in, prolong),
            ]
        )
    ]
    for load in loads:
        load.start()
    tm, sp = lax.axis_index("tm"), lax.axis_index("space")
    core, chip = lax.rem(tm, 2), tm // 2
    yh, z = lax.rem(chip, NY), chip // NY
    slices, parts = 2 * NY * NZ, 16

    def at(t=None, s=None):
        return {"tm": tm if t is None else t, "space": sp if s is None else s}

    other = 1 - core

    def chip_at(q, c):
        return at(2 * q + c)

    def y_at(k):
        return at((z * NY + lax.rem(yh + k + NY, NY)) * 2 + other)

    def z_at(k):
        return at(2 * (chip + NY * k) + other)

    def edge_at(target):
        return at(2 * ((z + 1) * NY + target) + other)

    def sp_at(k):
        return at(None, lax.rem(sp + k + parts, parts))

    sibling = at(tm + 1 - 2 * core)
    upper = at(lax.rem(tm + 1, slices))
    lower = at(lax.rem(tm + slices - 1, slices))

    def copy(src, dst, send, recv, to):
        return pltpu.make_async_remote_copy(
            src_ref=src, dst_ref=dst, send_sem=ssem.at[send], recv_sem=rsem.at[recv], device_id=to, device_id_type=MESH
        )

    def trace_copy(n):
        return copy(trace_out.at[n], trace_in.at[n], TRACE + n, TRACE + n, sp_at(1))

    def trace2_copy(n):
        return copy(trace_out.at[n], trace2_in.at[n], TRACE2 + n, TRACE2 + n, sp_at(2))

    def ahead_copy(n):
        return copy(ahead_out.at[n], ahead_in.at[n], AHEAD + n, AHEAD + n, sp_at(1))

    def nb_copy():
        return copy(nb_out, nb_in, SEM_NB, SEM_NB, sp_at(1))

    def send_trace(n, trace):
        trace_out[n] = trace
        trace2_copy(n).start()
        trace_copy(n).start()

    def s_copy(it):
        return copy(s_out.at[it], s_in.at[it], SEM_S + it, SEM_S + it, lower)

    def f_copy(it):
        return copy(f_out.at[it], f_pair.at[it, core], SEM_F + it, SEM_F + it, sibling)

    def late_copy():
        return copy(f_pair.at[1, 0], f_late, SEM_LATE, SEM_LATE, chip_at(chip + 1, core))

    def y_copy(it, k):
        if it == 0:
            slot, to = yh, y_at(k)
        else:
            slot = lax.rem(yh + 1, NY)
            to = at((chip // NY * NY + lax.rem(yh + k, NY) + NY * (yh // (NY - 1))) * 2 + other)
        return copy(t_out.at[it], t_all.at[it, slot], SEM_Y + NY * it + k, SEM_Y + NY * it + slot, to)

    def y_sends(it, act):
        for k in (2, 1, 3, 0):
            if it == 0:
                if k > 0:
                    act(y_copy(it, k))
            else:
                allowed = (yh == NY - 1) & (z < NZ - 1)
                if k > 0:
                    allowed = allowed | (yh < NY - 1)

                @pl.when(allowed)
                def _(k=k):
                    act(y_copy(it, k))

    def z_copy(it, k):
        sem = SEM_Z + (NZ - 1) * it + k - 1
        return copy(z_out.at[it], z_all.at[it, k - 1], sem, sem, z_at(k))

    def pre_copy(it):
        return copy(pre.at[it, other], pre.at[it, other], SEM_PRE + it, SEM_PRE + it, sibling)

    def p_copy(it):
        return copy(late.at[it, core], late.at[it, core], SEM_P + it, SEM_P + it, sibling)

    def q_copy(it, k):
        sem = SEM_Q + 3 * it + k - 1
        to = at(tm + 1 - 2 * core, lax.rem(sp + 4 * k, parts))
        return copy(q_out.at[it], q_all.at[it, k - 1], sem, sem, to)

    z_all[...] = jnp.zeros_like(z_all)
    t_all[1, 0] = jnp.zeros((COARSE, EL), f32)
    f_late[...] = jnp.zeros_like(f_late)
    late[...] = jnp.zeros_like(late)
    s_in[...] = jnp.zeros_like(s_in)

    chips = NY * NZ
    barrier = pltpu.get_barrier_semaphore()

    def tell(semaphore, device):
        pl.semaphore_signal(semaphore, inc=1, device_id=device, device_id_type=MESH)

    peers = [at(tm + 1 - 2 * core, lax.rem(sp + 4 * k, parts)) for k in (1, 2, 3)]
    for device in [sp_at(-1), sp_at(-2), sibling] + peers:
        tell(barrier, device)

    @pl.when(tm < slices - 1)
    def _():
        tell(barrier, upper)

    @pl.when(chip < chips - 1)
    def _():
        tell(barrier, chip_at(chip + 1, core))

    for k in range(1, NY):

        @pl.when(yh + k < NY)
        def _(k=k):
            tell(barrier, y_at(k))

    for k in range(1, NZ):

        @pl.when(z + k < NZ)
        def _(k=k):
            tell(barrier, z_at(k))

    last_y, first_y = yh // (NY - 1), 1 - yh // (NY - 1)

    @pl.when((yh == NY - 1) & (z < NZ - 1))
    def _():
        for target in range(NY - 1):
            tell(barrier, edge_at(target))

    heard = 6 + lax.min(tm, 1) + lax.min(chip, 1) + yh + z + first_y * lax.min(z, 1)

    def report():
        @pl.when(chip > 0)
        def _():
            tell(ready.at[2], chip_at(chip - 1, core))

        @pl.when((yh < NY - 1) & (z > 0))
        def _():
            tell(ready.at[3], at(2 * (z * NY - 1) + other))

        for k in range(1, NY):

            @pl.when(yh - k >= 0)
            def _(k=k):
                tell(ready.at[0], y_at(-k))

        for k in range(1, NZ):

            @pl.when(z - k >= 0)
            def _(k=k):
                tell(ready.at[1], z_at(-k))

    def hear(which, count):
        @pl.when(count > 0)
        def _():
            pl.semaphore_wait(ready.at[which], count)

    rows, cols = iota((NODES, NODES), 0), iota((NODES, NODES), 1)
    reorder = jnp.where(node_place(cols, rows), 1.0, 0.0)

    def reordered(flipped):
        return lax.dot_general(
            reorder, flipped, (((1,), (1,)), ((), ())), precision=highest, preferred_element_type=f32
        )

    loads[0].wait()
    for c in range(COMP):
        state[:, c * EL : (c + 1) * EL] = node_rows(guess, c * NODES)
    for load in loads[1:7]:
        load.wait()

    def sides(numbers, place):
        here = (numbers // EL) == jnp.broadcast_to(place, (1, EL))
        return numbers % EL, jnp.broadcast_to(here, (FACE, EL))

    index, own = sides(neighbors[...], sp)
    nb_out[...] = jnp.broadcast_to(neighbors[...].astype(f32), (8, EL))

    pl.semaphore_wait(barrier, heard)
    send_trace(0, state[0:FACE, :])
    nb_copy().start()
    report()

    volume = jnp.concatenate([node_rows(viscous), node_rows(deriv)], axis=0) * STEP
    gen3[...] = spread3(volume, node_place)
    lift_rows = reordered(lift[...]) * STEP
    lift3[...] = spread3(lift_rows, same)

    def volume_part(v, dest):
        yz = dot(gen3[...], stack3(v))
        for c in range(COMP):
            total = part(v, c) + part(yz[0:NODES], c)
            for d in range(COMP):
                total = total - jacobian[c, d] * part(yz[NODES:], d)
            dest[:, c * EL : (c + 1) * EL] = total

    def faces(jump):
        mixed = []
        for c in range(COMP):
            total = upwind[c, 0] * jump[0]
            for d in range(1, COMP):
                total = total + upwind[c, d] * jump[d]
            mixed.append(total)
        return stack3(jnp.concatenate(mixed, axis=1))

    def pair(n, side):
        last = n % PAIRS == PAIRS - 1
        v = state[...]
        volume_part(v, base)
        minus = [part(v[FACE : 2 * FACE], d) for d in range(COMP)]
        inner = [pick(part(v[0:FACE], d), index) for d in range(COMP)]
        known = faces([jnp.where(own, inner[d], 0.0) - minus[d] for d in range(COMP)])
        ahead_out[n] = base[0:FACE, :] + dot(lift3[0:FACE, :], known)
        ahead_copy(n).start()
        side()
        if n == 0:
            nb_copy().wait_recv()
        trace_copy(n).wait_recv()
        jump = [
            jnp.where(own, inner[d], pick(trace_in[n, :, d * EL : (d + 1) * EL], index)) - minus[d] for d in range(COMP)
        ]
        v = base[...] + dot(lift3[...], faces(jump))
        volume_part(v, base)
        if last:
            coarse_base = dot(rst3[...], stack3(base[...]))
        minus = [part(v[FACE : 2 * FACE], d) for d in range(COMP)]
        inner = [pick(part(v[0:FACE], d), index) for d in range(COMP)]
        index_before, own_before = sides(nb_in[0:1, :].astype(jnp.int32), lax.rem(sp + parts - 1, parts))
        trace2_copy(n).wait_recv()
        jump = [
            jnp.where(own_before, 0.0, pick(trace2_in[n, :, d * EL : (d + 1) * EL], index_before)) for d in range(COMP)
        ]
        missing = dot(lift3[0:FACE, :], faces(jump))
        ahead_copy(n).wait_recv()
        before = ahead_in[n] + missing
        jump = [jnp.where(own, inner[d], pick(part(before, d), index)) - minus[d] for d in range(COMP)]
        entering = faces(jump)
        if last:
            ends = coarse_base + dot(rl3[...], entering)
            state[...] = base[...] + dot(lift3[...], entering)
            return ends
        trace = base[0:FACE, :] + dot(lift3[0:FACE, :], entering)
        send_trace(n + 1, trace)
        state[0:FACE, :] = trace
        state[FACE:, :] = base[FACE:, :] + dot(lift3[FACE:, :], entering)

    def send_starts(it):
        s_out[it] = tall(dot(rst3[...], stack3(state[...])))

        @pl.when(tm > 0)
        def _():
            s_copy(it).start()

    def restriction():
        for load in loads[7:]:
            load.wait()
        full = restrict[...]
        rst3[...] = spread3(full, node_place)
        moved = dot32(full, jnp.where(node_place(rows, cols), 1.0, 0.0))
        rl3[...] = spread3(dot32(moved, lift_rows), same)
        send_starts(0)

    def orders():
        lane = iota((16, EL), 1)
        here = pick(coarse_map[...], sp * 8 + lane % 8)
        chosen = jnp.where(iota((16, EL), 0) == lane // 8, here.astype(f32), 0.0)
        member = jnp.sum(chosen, axis=0, keepdims=True) - jnp.broadcast_to(sp * EL, (1, EL)).astype(f32)
        grid = jnp.transpose(jnp.broadcast_to(member, (EL, EL)))
        hit = grid == iota((EL, EL), 1).astype(f32)
        back = jnp.sum(jnp.where(hit, iota((EL, EL), 0).astype(f32), 0.0), axis=0, keepdims=True)
        maps[0:8] = jnp.broadcast_to(member, (8, EL)).astype(jnp.int32)
        maps[8:16] = jnp.broadcast_to(back, (8, EL)).astype(jnp.int32)

    small = (COARSE, COARSE)
    second = jnp.broadcast_to(core, small) == 1
    eye = jnp.where(iota(small, 0) == iota(small, 1), 1.0, 0.0)
    zero = jnp.zeros(small, f32)

    def put(ref, value):
        high, low = halves(value)
        ref[0] = high
        ref[1] = low

    def beside(blocks):
        return jnp.concatenate(blocks, axis=1)

    def powers():
        a = self_ref[...]
        b = a + group_ref[...]
        put(w_t, jnp.concatenate([a, b], axis=0))
        for j, m in enumerate((a, b)):
            w = dot32(m, m)
            w2 = dot32(w, w)
            w_m[j, 0] = w
            w_m[j, 1] = w2
            w_m[j, 2] = dot32(w2, w)
            w_m[j, 3] = dot32(w2, w2)

    def by_yh(choices):
        place = jnp.broadcast_to(yh, small)
        value = choices[3]
        for j in (2, 1, 0):
            value = jnp.where(place == j, choices[j], value)
        return value

    def y_weights():
        w, w2, w3 = [jnp.where(second, w_m[0, j], w_m[1, j]) for j in range(3)]
        before = beside(
            [by_yh([zero, eye, w, w2]), by_yh([zero, zero, eye, w]), by_yh([zero, zero, zero, eye]), zero]
        )
        put(w_y, jnp.concatenate([before, beside([w3, w2, w, eye])], axis=0))

    def z_weights():
        w, w2, w3, w8 = [jnp.where(second, w_m[1, j], w_m[0, j]) for j in range(4)]
        weight = by_yh([eye, w, w2, w3])
        weights = [weight]
        for k in range(NZ - 2):
            weight = dot32(weight, w8)
            weights.append(weight)
        put(w_z, beside(weights))

    def q_weights():
        a, group = self_ref[...], group_ref[...]
        b = a + group
        aa, bb = w_m[0, 0], w_m[1, 0]
        even = beside([-0.25 * a, 0.25 * b, zero])
        odd = beside([-0.25 * aa, 0.25 * bb, 0.25 * group])
        even_own, odd_own = beside([a, zero, zero]), beside([aa, zero, a])
        here = jnp.broadcast_to(core, odd.shape) == 1
        mine, sent, own = jnp.where(here, odd, even), jnp.where(here, even, odd), jnp.where(here, odd_own, even_own)
        put(w_q, jnp.concatenate([mine, sent, own], axis=0))

    def chain(it, ends):
        @pl.when(tm < slices - 1)
        def _():
            s_copy(it).wait_recv()

        force = tall(ends) - s_in[it]
        f_out[it] = force
        f_copy(it).start()
        f_pair[it, core] = force
        copy(f_out.at[it], f_pair.at[it, other], SEM_F + it, SEM_F + it, sibling).wait_recv()
        both = dot3(w_t, f_pair[it, 0])
        first, other_chain = f_pair[it, 1] + both[0:COARSE], f_pair[it, 1] + both[COARSE:]
        is_second = jnp.broadcast_to(core, (COARSE, EL)) == 1
        t_out[it] = jnp.where(is_second, other_chain, first)
        kept = jnp.where(is_second, first, other_chain)
        if it == 0:
            hear(0, NY - 1 - yh)
            t_all[it, yh] = kept
        else:
            hear(3, (NY - 1) * last_y * lax.min(NZ - 1 - z, 1))

            @pl.when(yh < NY - 1)
            def _():
                t_all[it, lax.rem(yh + 1, NY)] = kept

        y_sends(it, lambda c: c.start())
        if it == 1:
            hear(2, lax.min(chips - 1 - chip, 1))

            @pl.when(chip < chips - 1)
            def _():
                late_copy().start()

        for j in range(NY):
            if it == 0:
                awaited = yh != j
            else:
                awaited = yh + 1 != j if j else z > 0

            @pl.when(awaited)
            def _(j=j):
                copy(t_out.at[it], t_all.at[it, j], SEM_Y, SEM_Y + NY * it + j, sibling).wait_recv()

        both = dot3(w_y, jnp.concatenate([t_all[it, j] for j in range(NY)], axis=0))
        z_out[it] = both[COARSE:]
        if it == 0:
            hear(1, NZ - 1 - z)
        for k in (4, 3, 5, 2, 6, 1, 7):

            @pl.when(z + k < NZ)
            def _(k=k):
                z_copy(it, k).start()

        pre[it, other] = both[0:COARSE]
        pre_copy(it).start()
        if it == 1:

            @pl.when(tm < slices - 2)
            def _():
                copy(state, fin, SEM_END, SEM_END, at(tm + 2)).start()

        @pl.when(z > 0)
        def _():
            for k in range(1, NZ):

                @pl.when(z >= k)
                def _(k=k):
                    z_copy(it, k).wait_recv()

            late[it, core] = dot3(w_z, jnp.concatenate([z_all[it, k] for k in range(NZ - 1)], axis=0))
            p_copy(it).start()

        copy(z_out.at[it], pre.at[it, core], SEM_PRE, SEM_PRE + it, sibling).wait_recv()
        if it == 1:

            @pl.when(chip > 0)
            def _():
                copy(z_out.at[it], f_late, SEM_LATE, SEM_LATE, sibling).wait_recv()

        @pl.when(z > 0)
        def _():
            copy(z_out.at[it], late.at[it, other], SEM_P, SEM_P + it, sibling).wait_recv()

        before = [pre[it, j] + late[it, j] for j in (0, 1)]
        stacked = jnp.concatenate(before + [f_pair[it, 0] if it == 0 else f_late[...]], axis=0)
        parts3 = dot3(w_q, stacked)
        q_out[it] = pick(parts3[COARSE : 2 * COARSE], maps[0:1])
        for k in (3, 1, 2):
            q_copy(it, k).start()
        mine = pick(parts3[0:COARSE], maps[0:1])
        for k in (2, 1, 3):
            q_copy(it, k).wait_recv()
        mean = (mine + q_all[it, 0]) + (q_all[it, 1] + q_all[it, 2])
        return wide(parts3[2 * COARSE :] + pick(mean, maps[8:9]))

    def after(*steps):
        for step in steps:
            step()

    tasks = [
        functools.partial(after, restriction, orders),
        powers,
        z_weights,
        functools.partial(after, y_weights, q_weights),
    ]
    for n in range(PAIRS):
        ends = pair(n, tasks[n])
    correction = chain(0, ends)
    raise_by = reordered(prolong[...])
    trace = state[0:FACE, :] + dot32(raise_by[0:FACE], correction)
    send_trace(PAIRS, trace)
    state[0:FACE, :] = trace
    state[FACE:, :] = state[FACE:, :] + dot32(raise_by[FACE:], correction)

    first_to_second = copy(cand, fin, SEM_END, SEM_END, sibling)

    @pl.when(tm == 0)
    def _():
        cand[...] = state[...]
        first_to_second.start()
        for c in range(COMP):
            fin[:, c * EL : (c + 1) * EL] = node_rows(guess, c * NODES)

    for n in range(PAIRS, 2 * PAIRS):
        ends = pair(n, functools.partial(send_starts, 1) if n == PAIRS else after)
    correction = chain(1, ends)
    added = dot32(raise_by, correction)

    @pl.when(tm > 0)
    def _():
        first_to_second.wait_recv()

    for c in range(COMP):
        for k, i in enumerate((3, 0, 1, 2)):
            rows = slice(k * FACE, (k + 1) * FACE)
            out[pl.ds(c * NODES + i, FACE, stride=4), :] = fin[rows, c * EL : (c + 1) * EL] + part(added[rows], c)

    nb_copy().wait_send()
    for n in range(2 * PAIRS):
        trace_copy(n).wait_send()
        trace2_copy(n).wait_send()
        ahead_copy(n).wait_send()
    for it in range(ITERS):

        @pl.when(tm > 0)
        def _(it=it):
            s_copy(it).wait_send()

        f_copy(it).wait_send()
        y_sends(it, lambda c: c.wait_send())
        pre_copy(it).wait_send()
        for k in (1, 2, 3):
            q_copy(it, k).wait_send()

        @pl.when(z > 0)
        def _(it=it):
            p_copy(it).wait_send()

        for k in range(1, NZ):

            @pl.when(z + k < NZ)
            def _(k=k, it=it):
                z_copy(it, k).wait_send()

    @pl.when(chip < chips - 1)
    def _():
        late_copy().wait_send()

    @pl.when(tm == 0)
    def _():
        first_to_second.wait_send()

    @pl.when(tm < slices - 2)
    def _():
        copy(state, fin, SEM_END, SEM_END + 0, sibling).wait_send()


def body(guess, deriv, viscous, jacobian, upwind, lift, restrict, prolong, coarse_self, coarse_group, neighbors, coarse_map):
    hbm = pl.BlockSpec(memory_space=pltpu.HBM)

    def buffer(*shape):
        return pltpu.VMEM(shape, f32)

    result = pl.pallas_call(
        kernel,
        out_shape=jax.ShapeDtypeStruct((COMP * NODES, EL), f32),
        in_specs=[hbm] * INPUTS,
        out_specs=pl.BlockSpec(memory_space=pltpu.VMEM),
        scratch_shapes=[
            buffer(COMP * NODES, EL),
            buffer(NODES, NODES),
            buffer(NODES, NODES),
            pltpu.SMEM((COMP, COMP), f32),
            pltpu.SMEM((COMP, COMP), f32),
            buffer(FACE, NODES),
            buffer(CNODES, NODES),
            buffer(CNODES, NODES),
            buffer(COARSE, COARSE),
            buffer(COARSE, COARSE),
            pltpu.VMEM((1, EL), jnp.int32),
            pltpu.VMEM((16, EL), jnp.int32),
            buffer(NODES, WIDE),
            buffer(NODES, WIDE),
            buffer(2 * PAIRS, FACE, WIDE),
            buffer(2 * PAIRS, FACE, WIDE),
            buffer(2 * PAIRS, FACE, WIDE),
            buffer(2 * PAIRS, FACE, WIDE),
            buffer(2 * PAIRS, FACE, WIDE),
            buffer(8, EL),
            buffer(8, EL),
            buffer(ITERS, COARSE, EL),
            buffer(ITERS, COARSE, EL),
            buffer(ITERS, COARSE, EL),
            buffer(ITERS, 2, COARSE, EL),
            buffer(COARSE, EL),
            buffer(ITERS, COARSE, EL),
            buffer(ITERS, NY, COARSE, EL),
            buffer(ITERS, COARSE, EL),
            buffer(ITERS, NZ - 1, COARSE, EL),
            buffer(ITERS, 2, COARSE, EL),
            buffer(ITERS, 2, COARSE, EL),
            buffer(ITERS, COARSE, EL),
            buffer(ITERS, 3, COARSE, EL),
            buffer(NODES, WIDE),
            buffer(NODES, WIDE),
            pltpu.VMEM((2 * NODES, 3 * NODES), bf16),
            pltpu.VMEM((NODES, 3 * FACE), bf16),
            pltpu.VMEM((CNODES, 3 * NODES), bf16),
            pltpu.VMEM((CNODES, 3 * FACE), bf16),
            buffer(2, 4, COARSE, COARSE),
            pltpu.VMEM((2, 2 * COARSE, COARSE), bf16),
            pltpu.VMEM((2, 2 * COARSE, NY * COARSE), bf16),
            pltpu.VMEM((2, COARSE, (NZ - 1) * COARSE), bf16),
            pltpu.VMEM((2, 3 * COARSE, 3 * COARSE), bf16),
            pltpu.VMEM((16, EL), jnp.int32),
            pltpu.SemaphoreType.DMA((SEMS,)),
            pltpu.SemaphoreType.DMA((SEMS,)),
            pltpu.SemaphoreType.DMA((INPUTS,)),
            pltpu.SemaphoreType.REGULAR((4,)),
        ],
        compiler_params=pltpu.CompilerParams(
            collective_id=0, has_side_effects=True, vmem_limit_bytes=60 * 2**20
        ),
        name="parareal",
    )(
        guess.reshape(COMP * NODES, EL), deriv, viscous, jacobian, upwind, lift.T, restrict, prolong.T,
        coarse_self, coarse_group, neighbors.reshape(1, EL), coarse_map.reshape(16, EL),
    )
    return result.reshape(1, COMP, NODES, EL)


def solution(mesh):
    return jax.shard_map(
        body,
        mesh=mesh,
        in_specs=(
            P("tm", None, None, "space"),
            P(), P(), P(), P(), P(), P(), P(), P(), P(),
            P("space"),
            P(),
        ),
        out_specs=P("tm", None, None, "space"),
        check_vma=False,
    )
```

```python
import functools

import jax
import jax.numpy as jnp
from jax import lax
from jax.experimental import pallas as pl
from jax.experimental.pallas import tpu as pltpu
from jax.sharding import PartitionSpec as P

COMP = 5
NODES = 64
FACE = 16
CNODES = 8
SUB = 8
ITERS = 2
COARSE = 40
EL = 128
WIDE = COMP * EL
NY = 4
NZ = 8
STEP = 0.08

f32 = jnp.float32
bf16 = jnp.bfloat16
highest = lax.Precision.HIGHEST
MESH = pl.DeviceIdType.MESH

PAIRS = SUB // 2
TRACE = 0
TRACE2 = TRACE + PAIRS * ITERS
AHEAD = TRACE2 + PAIRS * ITERS
SEM_NB = AHEAD + PAIRS * ITERS
SEM_S = SEM_NB + 1
SEM_F = SEM_S + ITERS
SEM_LATE = SEM_F + ITERS
SEM_Y = SEM_LATE + 1
SEM_Z = SEM_Y + NY * ITERS
SEM_PRE = SEM_Z + (NZ - 1) * ITERS
SEM_P = SEM_PRE + ITERS
SEM_Q = SEM_P + ITERS
SEM_END = SEM_Q + 3 * ITERS
SEMS = SEM_END + 1
INPUTS = 12


def iota(shape, dim):
    return lax.broadcasted_iota(jnp.int32, shape, dim)


def dot(a, b):
    return jnp.dot(a, b, preferred_element_type=f32)


def dot32(a, b):
    return jnp.dot(a, b, precision=highest, preferred_element_type=f32)


def dot3(weights, x):
    high, low = halves(x)
    return dot(weights[0], high) + (dot(weights[1], high) + dot(weights[0], low))


def halves(x):
    high = x.astype(bf16)
    return high, (x - high.astype(f32)).astype(bf16)


def stack3(x):
    high, low = halves(x)
    return jnp.concatenate([high, high, low], axis=0)


def stack_short(x):
    high = x.astype(bf16).astype(f32)
    return jnp.concatenate([high, high, x - high], axis=0).astype(bf16)


def spread3(x, place):
    depth = x.shape[1]
    rows, cols = iota((depth, 3 * depth), 0), iota((depth, 3 * depth), 1)
    third = cols // depth
    hit = place(rows, cols - third * depth)
    high, low = halves(x)
    outer = jnp.where(hit & (third != 1), 1.0, 0.0).astype(bf16)
    middle = jnp.where(hit & (third == 1), 1.0, 0.0).astype(bf16)
    return (dot(high, outer) + dot(low, middle)).astype(bf16)


def same(row, col):
    return row == col


def node_place(row, col):
    return row == (col % FACE) * 4 + (col // FACE + 3) % 4


def node_rows(ref, start=0):
    return jnp.concatenate(
        [ref[pl.ds(start + i, FACE, stride=4), :] for i in (3, 0, 1, 2)], axis=0
    )


def part(x, c):
    return x[:, c * EL : (c + 1) * EL]


def pick(x, index):
    return jnp.take_along_axis(x, jnp.broadcast_to(index, x.shape), axis=1, mode="promise_in_bounds")


def tall(x):
    return jnp.concatenate([part(x, c) for c in range(COMP)], axis=0)


def wide(x):
    return jnp.concatenate([x[c * CNODES : (c + 1) * CNODES] for c in range(COMP)], axis=1)


def kernel(
    guess_in, deriv_in, viscous_in, jacobian_in, upwind_in, lift_in, restrict_in, prolong_in, self_in, group_in,
    neighbors_in, coarse_map_in,
    out,
    guess, deriv, viscous, jacobian, upwind, lift, restrict, prolong, self_ref, group_ref, neighbors, coarse_map,
    state, base, trace_out, ahead_out, trace_in, trace2_in, ahead_in, nb_out, nb_in, s_out, s_in, f_out, f_pair, f_late, t_out, t_all, z_out, z_all, pre, late, q_out, q_all, cand, fin,
    gen3, lift3, rst3, rl3, pro3, w_m, w_t, w_y, w_z, w_q, maps,
    ssem, rsem, isem, ready,
):
    loads = [
        pltpu.make_async_copy(src, dst, isem.at[k])
        for k, (src, dst) in enumerate(
            [
                (guess_in, guess),
                (viscous_in, viscous),
                (deriv_in, deriv),
                (lift_in, lift),
                (neighbors_in, neighbors),
                (jacobian_in, jacobian),
                (upwind_in, upwind),
                (restrict_in, restrict),
                (self_in, self_ref),
                (group_in, group_ref),
                (coarse_map_in, coarse_map),
                (prolong_in, prolong),
            ]
        )
    ]
    for load in loads:
        load.start()
    tm, sp = lax.axis_index("tm"), lax.axis_index("space")
    core, chip = lax.rem(tm, 2), tm // 2
    yh, z = lax.rem(chip, NY), chip // NY
    slices, parts = 2 * NY * NZ, 16

    def at(t=None, s=None):
        return {"tm": tm if t is None else t, "space": sp if s is None else s}

    other = 1 - core

    def chip_at(q, c):
        return at(2 * q + c)

    def y_at(k):
        return at((z * NY + lax.rem(yh + k + NY, NY)) * 2 + other)

    def z_at(k):
        return at(2 * (chip + NY * k) + other)

    def edge_at(target):
        return at(2 * ((z + 1) * NY + target) + other)

    def sp_at(k):
        return at(None, lax.rem(sp + k + parts, parts))

    sibling = at(tm + 1 - 2 * core)
    upper = at(lax.rem(tm + 1, slices))
    lower = at(lax.rem(tm + slices - 1, slices))

    def copy(src, dst, send, recv, to):
        return pltpu.make_async_remote_copy(
            src_ref=src, dst_ref=dst, send_sem=ssem.at[send], recv_sem=rsem.at[recv], device_id=to, device_id_type=MESH
        )

    def trace_copy(n):
        return copy(trace_out.at[n], trace_in.at[n], TRACE + n, TRACE + n, sp_at(1))

    def trace2_copy(n):
        return copy(trace_out.at[n], trace2_in.at[n], TRACE2 + n, TRACE2 + n, sp_at(2))

    def ahead_copy(n):
        return copy(ahead_out.at[n], ahead_in.at[n], AHEAD + n, AHEAD + n, sp_at(1))

    def nb_copy():
        return copy(nb_out, nb_in, SEM_NB, SEM_NB, sp_at(1))

    def send_trace(n, trace):
        trace_out[n] = trace
        trace2_copy(n).start()
        trace_copy(n).start()

    def s_copy(it):
        return copy(s_out.at[it], s_in.at[it], SEM_S + it, SEM_S + it, lower)

    def f_copy(it):
        return copy(f_out.at[it], f_pair.at[it, core], SEM_F + it, SEM_F + it, sibling)

    def late_copy():
        return copy(f_pair.at[1, 0], f_late, SEM_LATE, SEM_LATE, chip_at(chip + 1, core))

    def y_copy(it, k):
        if it == 0:
            slot, to = yh, y_at(k)
        else:
            slot = lax.rem(yh + 1, NY)
            to = at((chip // NY * NY + lax.rem(yh + k, NY) + NY * (yh // (NY - 1))) * 2 + other)
        return copy(t_out.at[it], t_all.at[it, slot], SEM_Y + NY * it + k, SEM_Y + NY * it + slot, to)

    def y_sends(it, act):
        for k in (2, 1, 3, 0):
            if it == 0:
                if k > 0:
                    act(y_copy(it, k))
            else:
                allowed = (yh == NY - 1) & (z < NZ - 1)
                if k > 0:
                    allowed = allowed | (yh < NY - 1)

                @pl.when(allowed)
                def _(k=k):
                    act(y_copy(it, k))

    def z_copy(it, k):
        sem = SEM_Z + (NZ - 1) * it + k - 1
        return copy(z_out.at[it], z_all.at[it, k - 1], sem, sem, z_at(k))

    def pre_copy(it):
        return copy(pre.at[it, other], pre.at[it, other], SEM_PRE + it, SEM_PRE + it, sibling)

    def p_copy(it):
        return copy(late.at[it, core], late.at[it, core], SEM_P + it, SEM_P + it, sibling)

    def q_copy(it, k):
        sem = SEM_Q + 3 * it + k - 1
        to = at(tm + 1 - 2 * core, lax.rem(sp + 4 * k, parts))
        return copy(q_out.at[it], q_all.at[it, k - 1], sem, sem, to)

    z_all[...] = jnp.zeros_like(z_all)
    t_all[1, 0] = jnp.zeros((COARSE, EL), f32)
    f_late[...] = jnp.zeros_like(f_late)
    late[...] = jnp.zeros_like(late)
    s_in[...] = jnp.zeros_like(s_in)

    chips = NY * NZ
    barrier = pltpu.get_barrier_semaphore()

    def tell(semaphore, device):
        pl.semaphore_signal(semaphore, inc=1, device_id=device, device_id_type=MESH)

    peers = [at(tm + 1 - 2 * core, lax.rem(sp + 4 * k, parts)) for k in (1, 2, 3)]
    for device in [sp_at(-1), sp_at(-2), sibling] + peers:
        tell(barrier, device)

    @pl.when(tm < slices - 1)
    def _():
        tell(barrier, upper)

    @pl.when(chip < chips - 1)
    def _():
        tell(barrier, chip_at(chip + 1, core))

    for k in range(1, NY):

        @pl.when(yh + k < NY)
        def _(k=k):
            tell(barrier, y_at(k))

    for k in range(1, NZ):

        @pl.when(z + k < NZ)
        def _(k=k):
            tell(barrier, z_at(k))

    last_y, first_y = yh // (NY - 1), 1 - yh // (NY - 1)

    @pl.when((yh == NY - 1) & (z < NZ - 1))
    def _():
        for target in range(NY - 1):
            tell(barrier, edge_at(target))

    heard = 6 + lax.min(tm, 1) + lax.min(chip, 1) + yh + z + first_y * lax.min(z, 1)

    def report():
        @pl.when(chip > 0)
        def _():
            tell(ready.at[2], chip_at(chip - 1, core))

        @pl.when((yh < NY - 1) & (z > 0))
        def _():
            tell(ready.at[3], at(2 * (z * NY - 1) + other))

        for k in range(1, NY):

            @pl.when(yh - k >= 0)
            def _(k=k):
                tell(ready.at[0], y_at(-k))

        for k in range(1, NZ):

            @pl.when(z - k >= 0)
            def _(k=k):
                tell(ready.at[1], z_at(-k))

    def hear(which, count):
        @pl.when(count > 0)
        def _():
            pl.semaphore_wait(ready.at[which], count)

    rows, cols = iota((NODES, NODES), 0), iota((NODES, NODES), 1)
    reorder = jnp.where(node_place(cols, rows), 1.0, 0.0)

    def reordered(flipped):
        return lax.dot_general(
            reorder, flipped, (((1,), (1,)), ((), ())), precision=highest, preferred_element_type=f32
        )

    loads[0].wait()
    for c in range(COMP):
        state[:, c * EL : (c + 1) * EL] = node_rows(guess, c * NODES)
    for load in loads[1:7]:
        load.wait()

    def sides(numbers, place):
        here = (numbers // EL) == jnp.broadcast_to(place, (1, EL))
        return numbers % EL, jnp.broadcast_to(here, (FACE, EL))

    index, own = sides(neighbors[...], sp)
    nb_out[...] = jnp.broadcast_to(neighbors[...].astype(f32), (8, EL))

    pl.semaphore_wait(barrier, heard)
    send_trace(0, state[0:FACE, :])
    nb_copy().start()

    volume = jnp.concatenate([node_rows(viscous), node_rows(deriv)], axis=0) * STEP
    gen3[...] = spread3(volume, node_place)
    lift_rows = reordered(lift[...]) * STEP
    lift3[...] = spread3(lift_rows, same)

    def volume_part(v, dest):
        yz = dot(gen3[...], stack3(v))
        for c in range(COMP):
            total = part(v, c) + part(yz[0:NODES], c)
            for d in range(COMP):
                total = total - jacobian[c, d] * part(yz[NODES:], d)
            dest[:, c * EL : (c + 1) * EL] = total

    def faces(jump):
        mixed = []
        for c in range(COMP):
            total = upwind[c, 0] * jump[0]
            for d in range(1, COMP):
                total = total + upwind[c, d] * jump[d]
            mixed.append(total)
        return stack3(jnp.concatenate(mixed, axis=1))

    def pair(n, side):
        last = n % PAIRS == PAIRS - 1
        v = state[...]
        volume_part(v, base)
        minus = [part(v[FACE : 2 * FACE], d) for d in range(COMP)]
        inner = [pick(part(v[0:FACE], d), index) for d in range(COMP)]
        known = faces([jnp.where(own, inner[d], 0.0) - minus[d] for d in range(COMP)])
        ahead_out[n] = base[0:FACE, :] + dot(lift3[0:FACE, :], known)
        ahead_copy(n).start()
        side()
        if n == 0:
            nb_copy().wait_recv()
        trace_copy(n).wait_recv()
        jump = [
            jnp.where(own, inner[d], pick(trace_in[n, :, d * EL : (d + 1) * EL], index)) - minus[d] for d in range(COMP)
        ]
        v = base[...] + dot(lift3[...], faces(jump))
        volume_part(v, base)
        if last:
            coarse_base = dot(rst3[...], stack3(base[...]))
        minus = [part(v[FACE : 2 * FACE], d) for d in range(COMP)]
        inner = [pick(part(v[0:FACE], d), index) for d in range(COMP)]
        index_before, own_before = sides(nb_in[0:1, :].astype(jnp.int32), lax.rem(sp + parts - 1, parts))
        trace2_copy(n).wait_recv()
        jump = [
            jnp.where(own_before, 0.0, pick(trace2_in[n, :, d * EL : (d + 1) * EL], index_before)) for d in range(COMP)
        ]
        missing = dot(lift3[0:FACE, :], faces(jump))
        ahead_copy(n).wait_recv()
        before = ahead_in[n] + missing
        jump = [jnp.where(own, inner[d], pick(part(before, d), index)) - minus[d] for d in range(COMP)]
        entering = faces(jump)
        if last:
            ends = coarse_base + dot(rl3[...], entering)
            state[...] = base[...] + dot(lift3[...], entering)
            return ends
        trace = base[0:FACE, :] + dot(lift3[0:FACE, :], entering)
        send_trace(n + 1, trace)
        state[0:FACE, :] = trace
        state[FACE:, :] = base[FACE:, :] + dot(lift3[FACE:, :], entering)

    def send_starts(it):
        s_out[it] = tall(dot(rst3[...], stack3(state[...])))

        @pl.when(tm > 0)
        def _():
            s_copy(it).start()

    def restriction():
        for load in loads[7:]:
            load.wait()
        full = restrict[...]
        rst3[...] = spread3(full, node_place)
        pro3[...] = spread3(reordered(prolong[...]), same)
        moved = dot32(full, jnp.where(node_place(rows, cols), 1.0, 0.0))
        rl3[...] = spread3(dot32(moved, lift_rows), same)
        send_starts(0)

    def orders():
        lane = iota((16, EL), 1)
        here = pick(coarse_map[...], sp * 8 + lane % 8)
        chosen = jnp.where(iota((16, EL), 0) == lane // 8, here.astype(f32), 0.0)
        member = jnp.sum(chosen, axis=0, keepdims=True) - jnp.broadcast_to(sp * EL, (1, EL)).astype(f32)
        grid = jnp.transpose(jnp.broadcast_to(member, (EL, EL)))
        hit = grid == iota((EL, EL), 1).astype(f32)
        back = jnp.sum(jnp.where(hit, iota((EL, EL), 0).astype(f32), 0.0), axis=0, keepdims=True)
        maps[0:8] = jnp.broadcast_to(member, (8, EL)).astype(jnp.int32)
        maps[8:16] = jnp.broadcast_to(back, (8, EL)).astype(jnp.int32)

    small = (COARSE, COARSE)
    second = jnp.broadcast_to(core, small) == 1
    eye = jnp.where(iota(small, 0) == iota(small, 1), 1.0, 0.0)
    zero = jnp.zeros(small, f32)

    def put(ref, value):
        high, low = halves(value)
        ref[0] = high
        ref[1] = low

    def beside(blocks):
        return jnp.concatenate(blocks, axis=1)

    def powers():
        a = self_ref[...]
        b = a + group_ref[...]
        put(w_t, jnp.concatenate([a, b], axis=0))
        for j, m in enumerate((a, b)):
            w = dot32(m, m)
            w2 = dot32(w, w)
            w_m[j, 0] = w
            w_m[j, 1] = w2
            w_m[j, 2] = dot32(w2, w)
            w_m[j, 3] = dot32(w2, w2)

    def by_yh(choices):
        place = jnp.broadcast_to(yh, small)
        value = choices[3]
        for j in (2, 1, 0):
            value = jnp.where(place == j, choices[j], value)
        return value

    def y_weights():
        w, w2, w3 = [jnp.where(second, w_m[0, j], w_m[1, j]) for j in range(3)]
        before = beside(
            [by_yh([zero, eye, w, w2]), by_yh([zero, zero, eye, w]), by_yh([zero, zero, zero, eye]), zero]
        )
        put(w_y, jnp.concatenate([before, beside([w3, w2, w, eye])], axis=0))

    def z_weights():
        w, w2, w3, w8 = [jnp.where(second, w_m[1, j], w_m[0, j]) for j in range(4)]
        weight = by_yh([eye, w, w2, w3])
        weights = [weight]
        for k in range(NZ - 2):
            weight = dot32(weight, w8)
            weights.append(weight)
        put(w_z, beside(weights))

    def q_weights():
        a, group = self_ref[...], group_ref[...]
        b = a + group
        aa, bb = w_m[0, 0], w_m[1, 0]
        even = beside([-0.25 * a, 0.25 * b, zero])
        odd = beside([-0.25 * aa, 0.25 * bb, 0.25 * group])
        even_own, odd_own = beside([a, zero, zero]), beside([aa, zero, a])
        here = jnp.broadcast_to(core, odd.shape) == 1
        mine, sent, own = jnp.where(here, odd, even), jnp.where(here, even, odd), jnp.where(here, odd_own, even_own)
        put(w_q, jnp.concatenate([mine, sent, own], axis=0))

    def chain(it, ends):
        @pl.when(tm < slices - 1)
        def _():
            s_copy(it).wait_recv()

        force = tall(ends) - s_in[it]
        f_out[it] = force
        f_copy(it).start()
        f_pair[it, core] = force
        copy(f_out.at[it], f_pair.at[it, other], SEM_F + it, SEM_F + it, sibling).wait_recv()
        both = dot3(w_t, f_pair[it, 0])
        first, other_chain = f_pair[it, 1] + both[0:COARSE], f_pair[it, 1] + both[COARSE:]
        is_second = jnp.broadcast_to(core, (COARSE, EL)) == 1
        t_out[it] = jnp.where(is_second, other_chain, first)
        kept = jnp.where(is_second, first, other_chain)
        if it == 0:
            hear(0, NY - 1 - yh)
            t_all[it, yh] = kept
        else:
            hear(3, (NY - 1) * last_y * lax.min(NZ - 1 - z, 1))

            @pl.when(yh < NY - 1)
            def _():
                t_all[it, lax.rem(yh + 1, NY)] = kept

        y_sends(it, lambda c: c.start())
        if it == 1:
            hear(2, lax.min(chips - 1 - chip, 1))

            @pl.when(chip < chips - 1)
            def _():
                late_copy().start()

        for j in range(NY):
            if it == 0:
                awaited = yh != j
            else:
                awaited = yh + 1 != j if j else z > 0

            @pl.when(awaited)
            def _(j=j):
                copy(t_out.at[it], t_all.at[it, j], SEM_Y, SEM_Y + NY * it + j, sibling).wait_recv()

        both = dot3(w_y, jnp.concatenate([t_all[it, j] for j in range(NY)], axis=0))
        z_out[it] = both[COARSE:]
        if it == 0:
            hear(1, NZ - 1 - z)
        for k in range(1, NZ):

            @pl.when(z + k < NZ)
            def _(k=k):
                z_copy(it, k).start()

        pre[it, other] = both[0:COARSE]
        pre_copy(it).start()
        if it == 1:

            @pl.when(tm < slices - 2)
            def _():
                copy(state, fin, SEM_END, SEM_END, at(tm + 2)).start()

        @pl.when(z > 0)
        def _():
            for k in range(1, NZ):

                @pl.when(z >= k)
                def _(k=k):
                    z_copy(it, k).wait_recv()

            late[it, core] = dot3(w_z, jnp.concatenate([z_all[it, k] for k in range(NZ - 1)], axis=0))
            p_copy(it).start()

        copy(z_out.at[it], pre.at[it, core], SEM_PRE, SEM_PRE + it, sibling).wait_recv()
        if it == 1:

            @pl.when(chip > 0)
            def _():
                copy(z_out.at[it], f_late, SEM_LATE, SEM_LATE, sibling).wait_recv()

        @pl.when(z > 0)
        def _():
            copy(z_out.at[it], late.at[it, other], SEM_P, SEM_P + it, sibling).wait_recv()

        before = [pre[it, j] + late[it, j] for j in (0, 1)]
        stacked = jnp.concatenate(before + [f_pair[it, 0] if it == 0 else f_late[...]], axis=0)
        parts3 = dot3(w_q, stacked)
        q_out[it] = pick(parts3[COARSE : 2 * COARSE], maps[0:1])
        for k in (3, 1, 2):
            q_copy(it, k).start()
        mine = pick(parts3[0:COARSE], maps[0:1])
        for k in (2, 1, 3):
            q_copy(it, k).wait_recv()
        mean = (mine + q_all[it, 0]) + (q_all[it, 1] + q_all[it, 2])
        return wide(parts3[2 * COARSE :] + pick(mean, maps[8:9]))

    def after(*steps):
        for step in steps:
            step()

    tasks = [
        functools.partial(after, report, restriction, orders),
        powers,
        z_weights,
        functools.partial(after, y_weights, q_weights),
    ]
    for n in range(PAIRS):
        ends = pair(n, tasks[n])
    correction = chain(0, ends)
    rising = stack_short(correction)
    trace = state[0:FACE, :] + dot(pro3[0:FACE, :], rising)
    send_trace(PAIRS, trace)
    state[0:FACE, :] = trace
    state[FACE:, :] = state[FACE:, :] + dot(pro3[FACE:, :], rising)

    first_to_second = copy(cand, fin, SEM_END, SEM_END, sibling)

    @pl.when(tm == 0)
    def _():
        cand[...] = state[...]
        first_to_second.start()
        for c in range(COMP):
            fin[:, c * EL : (c + 1) * EL] = node_rows(guess, c * NODES)

    for n in range(PAIRS, 2 * PAIRS):
        ends = pair(n, functools.partial(send_starts, 1) if n == PAIRS else after)
    correction = chain(1, ends)
    added = dot(pro3[...], stack_short(correction))

    @pl.when(tm > 0)
    def _():
        first_to_second.wait_recv()

    for c in range(COMP):
        for k, i in enumerate((3, 0, 1, 2)):
            rows = slice(k * FACE, (k + 1) * FACE)
            out[pl.ds(c * NODES + i, FACE, stride=4), :] = fin[rows, c * EL : (c + 1) * EL] + part(added[rows], c)

    nb_copy().wait_send()
    for n in range(2 * PAIRS):
        trace_copy(n).wait_send()
        trace2_copy(n).wait_send()
        ahead_copy(n).wait_send()
    for it in range(ITERS):

        @pl.when(tm > 0)
        def _(it=it):
            s_copy(it).wait_send()

        f_copy(it).wait_send()
        y_sends(it, lambda c: c.wait_send())
        pre_copy(it).wait_send()
        for k in (1, 2, 3):
            q_copy(it, k).wait_send()

        @pl.when(z > 0)
        def _(it=it):
            p_copy(it).wait_send()

        for k in range(1, NZ):

            @pl.when(z + k < NZ)
            def _(k=k, it=it):
                z_copy(it, k).wait_send()

    @pl.when(chip < chips - 1)
    def _():
        late_copy().wait_send()

    @pl.when(tm == 0)
    def _():
        first_to_second.wait_send()

    @pl.when(tm < slices - 2)
    def _():
        copy(state, fin, SEM_END, SEM_END + 0, sibling).wait_send()


def body(guess, deriv, viscous, jacobian, upwind, lift, restrict, prolong, coarse_self, coarse_group, neighbors, coarse_map):
    hbm = pl.BlockSpec(memory_space=pltpu.HBM)

    def buffer(*shape):
        return pltpu.VMEM(shape, f32)

    result = pl.pallas_call(
        kernel,
        out_shape=jax.ShapeDtypeStruct((COMP * NODES, EL), f32),
        in_specs=[hbm] * INPUTS,
        out_specs=pl.BlockSpec(memory_space=pltpu.VMEM),
        scratch_shapes=[
            buffer(COMP * NODES, EL),
            buffer(NODES, NODES),
            buffer(NODES, NODES),
            pltpu.SMEM((COMP, COMP), f32),
            pltpu.SMEM((COMP, COMP), f32),
            buffer(FACE, NODES),
            buffer(CNODES, NODES),
            buffer(CNODES, NODES),
            buffer(COARSE, COARSE),
            buffer(COARSE, COARSE),
            pltpu.VMEM((1, EL), jnp.int32),
            pltpu.VMEM((16, EL), jnp.int32),
            buffer(NODES, WIDE),
            buffer(NODES, WIDE),
            buffer(2 * PAIRS, FACE, WIDE),
            buffer(2 * PAIRS, FACE, WIDE),
            buffer(2 * PAIRS, FACE, WIDE),
            buffer(2 * PAIRS, FACE, WIDE),
            buffer(2 * PAIRS, FACE, WIDE),
            buffer(8, EL),
            buffer(8, EL),
            buffer(ITERS, COARSE, EL),
            buffer(ITERS, COARSE, EL),
            buffer(ITERS, COARSE, EL),
            buffer(ITERS, 2, COARSE, EL),
            buffer(COARSE, EL),
            buffer(ITERS, COARSE, EL),
            buffer(ITERS, NY, COARSE, EL),
            buffer(ITERS, COARSE, EL),
            buffer(ITERS, NZ - 1, COARSE, EL),
            buffer(ITERS, 2, COARSE, EL),
            buffer(ITERS, 2, COARSE, EL),
            buffer(ITERS, COARSE, EL),
            buffer(ITERS, 3, COARSE, EL),
            buffer(NODES, WIDE),
            buffer(NODES, WIDE),
            pltpu.VMEM((2 * NODES, 3 * NODES), bf16),
            pltpu.VMEM((NODES, 3 * FACE), bf16),
            pltpu.VMEM((CNODES, 3 * NODES), bf16),
            pltpu.VMEM((CNODES, 3 * FACE), bf16),
            pltpu.VMEM((NODES, 3 * CNODES), bf16),
            buffer(2, 4, COARSE, COARSE),
            pltpu.VMEM((2, 2 * COARSE, COARSE), bf16),
            pltpu.VMEM((2, 2 * COARSE, NY * COARSE), bf16),
            pltpu.VMEM((2, COARSE, (NZ - 1) * COARSE), bf16),
            pltpu.VMEM((2, 3 * COARSE, 3 * COARSE), bf16),
            pltpu.VMEM((16, EL), jnp.int32),
            pltpu.SemaphoreType.DMA((SEMS,)),
            pltpu.SemaphoreType.DMA((SEMS,)),
            pltpu.SemaphoreType.DMA((INPUTS,)),
            pltpu.SemaphoreType.REGULAR((4,)),
        ],
        compiler_params=pltpu.CompilerParams(
            collective_id=0, has_side_effects=True, vmem_limit_bytes=60 * 2**20
        ),
        name="parareal",
    )(
        guess.reshape(COMP * NODES, EL), deriv, viscous, jacobian, upwind, lift.T, restrict, prolong.T,
        coarse_self, coarse_group, neighbors.reshape(1, EL), coarse_map.reshape(16, EL),
    )
    return result.reshape(1, COMP, NODES, EL)


def solution(mesh):
    return jax.shard_map(
        body,
        mesh=mesh,
        in_specs=(
            P("tm", None, None, "space"),
            P(), P(), P(), P(), P(), P(), P(), P(), P(),
            P("space"),
            P(),
        ),
        out_specs=P("tm", None, None, "space"),
        check_vma=False,
    )
```

```python
import functools

import jax
import jax.numpy as jnp
from jax import lax
from jax.experimental import pallas as pl
from jax.experimental.pallas import tpu as pltpu
from jax.sharding import PartitionSpec as P

COMP = 5
NODES = 64
FACE = 16
CNODES = 8
SUB = 8
ITERS = 2
COARSE = 40
EL = 128
WIDE = COMP * EL
NY = 4
NZ = 8
STEP = 0.08

f32 = jnp.float32
bf16 = jnp.bfloat16
highest = lax.Precision.HIGHEST
MESH = pl.DeviceIdType.MESH

PAIRS = SUB // 2
TRACE = 0
TRACE2 = TRACE + PAIRS * ITERS
AHEAD = TRACE2 + PAIRS * ITERS
SEM_NB = AHEAD + PAIRS * ITERS
SEM_S = SEM_NB + 1
SEM_F = SEM_S + ITERS
SEM_LATE = SEM_F + ITERS
SEM_Y = SEM_LATE + 1
SEM_Z = SEM_Y + NY * ITERS
SEM_PRE = SEM_Z + (NZ - 1) * ITERS
SEM_P = SEM_PRE + ITERS
SEM_Q = SEM_P + ITERS
SEM_END = SEM_Q + 3 * ITERS
SEMS = SEM_END + 1
INPUTS = 12


def iota(shape, dim):
    return lax.broadcasted_iota(jnp.int32, shape, dim)


def dot(a, b):
    return jnp.dot(a, b, preferred_element_type=f32)


def dot32(a, b):
    return jnp.dot(a, b, precision=highest, preferred_element_type=f32)


def dot3(weights, x):
    high, low = halves(x)
    return dot(weights[0], high) + (dot(weights[1], high) + dot(weights[0], low))


def halves(x):
    high = x.astype(bf16)
    return high, (x - high.astype(f32)).astype(bf16)


def stack3(x):
    high, low = halves(x)
    return jnp.concatenate([high, high, low], axis=0)


def stack_short(x):
    high = x.astype(bf16).astype(f32)
    return jnp.concatenate([high, high, x - high], axis=0).astype(bf16)


def spread3(x, place):
    depth = x.shape[1]
    rows, cols = iota((depth, 3 * depth), 0), iota((depth, 3 * depth), 1)
    third = cols // depth
    hit = place(rows, cols - third * depth)
    high, low = halves(x)
    outer = jnp.where(hit & (third != 1), 1.0, 0.0).astype(bf16)
    middle = jnp.where(hit & (third == 1), 1.0, 0.0).astype(bf16)
    return (dot(high, outer) + dot(low, middle)).astype(bf16)


def same(row, col):
    return row == col


def node_place(row, col):
    return row == (col % FACE) * 4 + (col // FACE + 3) % 4


def node_rows(ref, start=0):
    return jnp.concatenate(
        [ref[pl.ds(start + i, FACE, stride=4), :] for i in (3, 0, 1, 2)], axis=0
    )


def part(x, c):
    return x[:, c * EL : (c + 1) * EL]


def pick(x, index):
    return jnp.take_along_axis(x, jnp.broadcast_to(index, x.shape), axis=1, mode="promise_in_bounds")


def tall(x):
    return jnp.concatenate([part(x, c) for c in range(COMP)], axis=0)


def wide(x):
    return jnp.concatenate([x[c * CNODES : (c + 1) * CNODES] for c in range(COMP)], axis=1)


def kernel(
    guess_in, deriv_in, viscous_in, jacobian_in, upwind_in, lift_in, restrict_in, prolong_in, self_in, group_in,
    neighbors_in, coarse_map_in,
    out,
    guess, deriv, viscous, jacobian, upwind, lift, restrict, prolong, self_ref, group_ref, neighbors, coarse_map,
    state, base, trace_out, ahead_out, trace_in, trace2_in, ahead_in, nb_out, nb_in, s_out, s_in, f_out, f_pair, f_late, t_out, t_all, z_out, z_all, pre, late, q_out, q_all, cand, fin,
    gen3, lift3, rst3, rl3, pro3, w_m, w_t, w_y, w_z, w_q, maps,
    ssem, rsem, isem, ready,
):
    loads = [
        pltpu.make_async_copy(src, dst, isem.at[k])
        for k, (src, dst) in enumerate(
            [
                (guess_in, guess),
                (viscous_in, viscous),
                (deriv_in, deriv),
                (lift_in, lift),
                (neighbors_in, neighbors),
                (jacobian_in, jacobian),
                (upwind_in, upwind),
                (restrict_in, restrict),
                (self_in, self_ref),
                (group_in, group_ref),
                (coarse_map_in, coarse_map),
                (prolong_in, prolong),
            ]
        )
    ]
    for load in loads:
        load.start()
    tm, sp = lax.axis_index("tm"), lax.axis_index("space")
    core, chip = lax.rem(tm, 2), tm // 2
    yh, z = lax.rem(chip, NY), chip // NY
    slices, parts = 2 * NY * NZ, 16

    def at(t=None, s=None):
        return {"tm": tm if t is None else t, "space": sp if s is None else s}

    other = 1 - core

    def chip_at(q, c):
        return at(2 * q + c)

    def y_at(k):
        return at((z * NY + lax.rem(yh + k + NY, NY)) * 2 + other)

    def z_at(k):
        return at(2 * (chip + NY * k) + other)

    def edge_at(target):
        return at(2 * ((z + 1) * NY + target) + other)

    def sp_at(k):
        return at(None, lax.rem(sp + k + parts, parts))

    sibling = at(tm + 1 - 2 * core)
    upper = at(lax.rem(tm + 1, slices))
    lower = at(lax.rem(tm + slices - 1, slices))

    def copy(src, dst, send, recv, to):
        return pltpu.make_async_remote_copy(
            src_ref=src, dst_ref=dst, send_sem=ssem.at[send], recv_sem=rsem.at[recv], device_id=to, device_id_type=MESH
        )

    def trace_copy(n):
        return copy(trace_out.at[n], trace_in.at[n], TRACE + n, TRACE + n, sp_at(1))

    def trace2_copy(n):
        return copy(trace_out.at[n], trace2_in.at[n], TRACE2 + n, TRACE2 + n, sp_at(2))

    def ahead_copy(n):
        return copy(ahead_out.at[n], ahead_in.at[n], AHEAD + n, AHEAD + n, sp_at(1))

    def nb_copy():
        return copy(nb_out, nb_in, SEM_NB, SEM_NB, sp_at(1))

    def send_trace(n, trace):
        trace_out[n] = trace
        trace2_copy(n).start()
        trace_copy(n).start()

    def s_copy(it):
        return copy(s_out.at[it], s_in.at[it], SEM_S + it, SEM_S + it, lower)

    def f_copy(it):
        return copy(f_out.at[it], f_pair.at[it, core], SEM_F + it, SEM_F + it, sibling)

    def late_copy():
        return copy(f_pair.at[1, 0], f_late, SEM_LATE, SEM_LATE, chip_at(chip + 1, core))

    def y_copy(it, k):
        if it == 0:
            slot, to = yh, y_at(k)
        else:
            slot = lax.rem(yh + 1, NY)
            to = at((chip // NY * NY + lax.rem(yh + k, NY) + NY * (yh // (NY - 1))) * 2 + other)
        return copy(t_out.at[it], t_all.at[it, slot], SEM_Y + NY * it + k, SEM_Y + NY * it + slot, to)

    def y_sends(it, act):
        for k in (2, 1, 3, 0):
            if it == 0:
                if k > 0:
                    act(y_copy(it, k))
            else:
                allowed = (yh == NY - 1) & (z < NZ - 1)
                if k > 0:
                    allowed = allowed | (yh < NY - 1)

                @pl.when(allowed)
                def _(k=k):
                    act(y_copy(it, k))

    def z_copy(it, k):
        sem = SEM_Z + (NZ - 1) * it + k - 1
        return copy(z_out.at[it], z_all.at[it, k - 1], sem, sem, z_at(k))

    def pre_copy(it):
        return copy(pre.at[it, other], pre.at[it, other], SEM_PRE + it, SEM_PRE + it, sibling)

    def p_copy(it):
        return copy(late.at[it, core], late.at[it, core], SEM_P + it, SEM_P + it, sibling)

    def q_copy(it, k):
        sem = SEM_Q + 3 * it + k - 1
        to = at(tm + 1 - 2 * core, lax.rem(sp + 4 * k, parts))
        return copy(q_out.at[it], q_all.at[it, k - 1], sem, sem, to)

    z_all[...] = jnp.zeros_like(z_all)
    t_all[1, 0] = jnp.zeros((COARSE, EL), f32)
    f_late[...] = jnp.zeros_like(f_late)
    late[...] = jnp.zeros_like(late)
    s_in[...] = jnp.zeros_like(s_in)

    chips = NY * NZ
    barrier = pltpu.get_barrier_semaphore()

    def tell(semaphore, device):
        pl.semaphore_signal(semaphore, inc=1, device_id=device, device_id_type=MESH)

    peers = [at(tm + 1 - 2 * core, lax.rem(sp + 4 * k, parts)) for k in (1, 2, 3)]
    for device in [sp_at(-1), sp_at(-2), sibling] + peers:
        tell(barrier, device)

    @pl.when(tm < slices - 1)
    def _():
        tell(barrier, upper)

    @pl.when(chip < chips - 1)
    def _():
        tell(barrier, chip_at(chip + 1, core))

    for k in range(1, NY):

        @pl.when(yh + k < NY)
        def _(k=k):
            tell(barrier, y_at(k))

    for k in range(1, NZ):

        @pl.when(z + k < NZ)
        def _(k=k):
            tell(barrier, z_at(k))

    last_y, first_y = yh // (NY - 1), 1 - yh // (NY - 1)

    @pl.when((yh == NY - 1) & (z < NZ - 1))
    def _():
        for target in range(NY - 1):
            tell(barrier, edge_at(target))

    heard = 6 + lax.min(tm, 1) + lax.min(chip, 1) + yh + z + first_y * lax.min(z, 1)

    def report():
        @pl.when(chip > 0)
        def _():
            tell(ready.at[2], chip_at(chip - 1, core))

        @pl.when((yh < NY - 1) & (z > 0))
        def _():
            tell(ready.at[3], at(2 * (z * NY - 1) + other))

        for k in range(1, NY):

            @pl.when(yh - k >= 0)
            def _(k=k):
                tell(ready.at[0], y_at(-k))

        for k in range(1, NZ):

            @pl.when(z - k >= 0)
            def _(k=k):
                tell(ready.at[1], z_at(-k))

    def hear(which, count):
        @pl.when(count > 0)
        def _():
            pl.semaphore_wait(ready.at[which], count)

    rows, cols = iota((NODES, NODES), 0), iota((NODES, NODES), 1)
    reorder = jnp.where(node_place(cols, rows), 1.0, 0.0)

    def reordered(flipped):
        return lax.dot_general(
            reorder, flipped, (((1,), (1,)), ((), ())), precision=highest, preferred_element_type=f32
        )

    loads[0].wait()
    for c in range(COMP):
        state[:, c * EL : (c + 1) * EL] = node_rows(guess, c * NODES)
    for load in loads[1:7]:
        load.wait()

    def sides(numbers, place):
        here = (numbers // EL) == jnp.broadcast_to(place, (1, EL))
        return numbers % EL, jnp.broadcast_to(here, (FACE, EL))

    index, own = sides(neighbors[...], sp)
    nb_out[...] = jnp.broadcast_to(neighbors[...].astype(f32), (8, EL))

    pl.semaphore_wait(barrier, heard)
    send_trace(0, state[0:FACE, :])
    nb_copy().start()

    volume = jnp.concatenate([node_rows(viscous), node_rows(deriv)], axis=0) * STEP
    gen3[...] = spread3(volume, node_place)
    lift_rows = reordered(lift[...]) * STEP
    lift3[...] = spread3(lift_rows, same)

    def volume_part(v, dest):
        yz = dot(gen3[...], stack3(v))
        for c in range(COMP):
            total = part(v, c) + part(yz[0:NODES], c)
            for d in range(COMP):
                total = total - jacobian[c, d] * part(yz[NODES:], d)
            dest[:, c * EL : (c + 1) * EL] = total

    def faces(jump):
        mixed = []
        for c in range(COMP):
            total = upwind[c, 0] * jump[0]
            for d in range(1, COMP):
                total = total + upwind[c, d] * jump[d]
            mixed.append(total)
        return stack3(jnp.concatenate(mixed, axis=1))

    def pair(n, side):
        last = n % PAIRS == PAIRS - 1
        v = state[...]
        volume_part(v, base)
        minus = [part(v[FACE : 2 * FACE], d) for d in range(COMP)]
        inner = [pick(part(v[0:FACE], d), index) for d in range(COMP)]
        known = faces([jnp.where(own, inner[d], 0.0) - minus[d] for d in range(COMP)])
        ahead_out[n] = base[0:FACE, :] + dot(lift3[0:FACE, :], known)
        ahead_copy(n).start()
        side()
        if n == 0:
            nb_copy().wait_recv()
        trace_copy(n).wait_recv()
        jump = [
            jnp.where(own, inner[d], pick(trace_in[n, :, d * EL : (d + 1) * EL], index)) - minus[d] for d in range(COMP)
        ]
        v = base[...] + dot(lift3[...], faces(jump))
        volume_part(v, base)
        if last:
            coarse_base = dot(rst3[...], stack3(base[...]))
        minus = [part(v[FACE : 2 * FACE], d) for d in range(COMP)]
        inner = [pick(part(v[0:FACE], d), index) for d in range(COMP)]
        index_before, own_before = sides(nb_in[0:1, :].astype(jnp.int32), lax.rem(sp + parts - 1, parts))
        trace2_copy(n).wait_recv()
        jump = [
            jnp.where(own_before, 0.0, pick(trace2_in[n, :, d * EL : (d + 1) * EL], index_before)) for d in range(COMP)
        ]
        missing = dot(lift3[0:FACE, :], faces(jump))
        ahead_copy(n).wait_recv()
        before = ahead_in[n] + missing
        jump = [jnp.where(own, inner[d], pick(part(before, d), index)) - minus[d] for d in range(COMP)]
        entering = faces(jump)
        if last:
            ends = coarse_base + dot(rl3[...], entering)
            state[...] = base[...] + dot(lift3[...], entering)
            return ends
        trace = base[0:FACE, :] + dot(lift3[0:FACE, :], entering)
        send_trace(n + 1, trace)
        state[0:FACE, :] = trace
        state[FACE:, :] = base[FACE:, :] + dot(lift3[FACE:, :], entering)

    def send_starts(it):
        s_out[it] = tall(dot(rst3[...], stack3(state[...])))

        @pl.when(tm > 0)
        def _():
            s_copy(it).start()

    def restriction():
        for load in loads[7:]:
            load.wait()
        full = restrict[...]
        rst3[...] = spread3(full, node_place)
        pro3[...] = spread3(reordered(prolong[...]), same)
        moved = dot32(full, jnp.where(node_place(rows, cols), 1.0, 0.0))
        rl3[...] = spread3(dot32(moved, lift_rows), same)
        send_starts(0)

    def orders():
        lane = iota((16, EL), 1)
        here = pick(coarse_map[...], sp * 8 + lane % 8)
        chosen = jnp.where(iota((16, EL), 0) == lane // 8, here.astype(f32), 0.0)
        member = jnp.sum(chosen, axis=0, keepdims=True) - jnp.broadcast_to(sp * EL, (1, EL)).astype(f32)
        grid = jnp.transpose(jnp.broadcast_to(member, (EL, EL)))
        hit = grid == iota((EL, EL), 1).astype(f32)
        back = jnp.sum(jnp.where(hit, iota((EL, EL), 0).astype(f32), 0.0), axis=0, keepdims=True)
        maps[0:8] = jnp.broadcast_to(member, (8, EL)).astype(jnp.int32)
        maps[8:16] = jnp.broadcast_to(back, (8, EL)).astype(jnp.int32)

    small = (COARSE, COARSE)
    second = jnp.broadcast_to(core, small) == 1
    eye = jnp.where(iota(small, 0) == iota(small, 1), 1.0, 0.0)
    zero = jnp.zeros(small, f32)

    def put(ref, value):
        high, low = halves(value)
        ref[0] = high
        ref[1] = low

    def beside(blocks):
        return jnp.concatenate(blocks, axis=1)

    def powers():
        a = self_ref[...]
        b = a + group_ref[...]
        put(w_t, jnp.concatenate([a, b], axis=0))
        for j, m in enumerate((a, b)):
            w = dot32(m, m)
            w2 = dot32(w, w)
            w_m[j, 0] = w
            w_m[j, 1] = w2
            w_m[j, 2] = dot32(w2, w)
            w_m[j, 3] = dot32(w2, w2)

    def by_yh(choices):
        place = jnp.broadcast_to(yh, small)
        value = choices[3]
        for j in (2, 1, 0):
            value = jnp.where(place == j, choices[j], value)
        return value

    def y_weights():
        w, w2, w3 = [jnp.where(second, w_m[0, j], w_m[1, j]) for j in range(3)]
        before = beside(
            [by_yh([zero, eye, w, w2]), by_yh([zero, zero, eye, w]), by_yh([zero, zero, zero, eye]), zero]
        )
        put(w_y, jnp.concatenate([before, beside([w3, w2, w, eye])], axis=0))

    def z_weights():
        w, w2, w3, w8 = [jnp.where(second, w_m[1, j], w_m[0, j]) for j in range(4)]
        weight = by_yh([eye, w, w2, w3])
        weights = [weight]
        for k in range(NZ - 2):
            weight = dot32(weight, w8)
            weights.append(weight)
        put(w_z, beside(weights))

    def q_weights():
        a, group = self_ref[...], group_ref[...]
        b = a + group
        aa, bb = w_m[0, 0], w_m[1, 0]
        even = beside([-0.25 * a, 0.25 * b, zero])
        odd = beside([-0.25 * aa, 0.25 * bb, 0.25 * group])
        even_own, odd_own = beside([a, zero, zero]), beside([aa, zero, a])
        here = jnp.broadcast_to(core, odd.shape) == 1
        mine, sent, own = jnp.where(here, odd, even), jnp.where(here, even, odd), jnp.where(here, odd_own, even_own)
        put(w_q, jnp.concatenate([mine, sent, own], axis=0))

    def chain(it, ends):
        @pl.when(tm < slices - 1)
        def _():
            s_copy(it).wait_recv()

        force = tall(ends) - s_in[it]
        f_out[it] = force
        f_copy(it).start()
        f_pair[it, core] = force
        copy(f_out.at[it], f_pair.at[it, other], SEM_F + it, SEM_F + it, sibling).wait_recv()
        both = dot3(w_t, f_pair[it, 0])
        first, other_chain = f_pair[it, 1] + both[0:COARSE], f_pair[it, 1] + both[COARSE:]
        is_second = jnp.broadcast_to(core, (COARSE, EL)) == 1
        t_out[it] = jnp.where(is_second, other_chain, first)
        kept = jnp.where(is_second, first, other_chain)
        if it == 0:
            hear(0, NY - 1 - yh)
            t_all[it, yh] = kept
        else:
            hear(3, (NY - 1) * last_y * lax.min(NZ - 1 - z, 1))

            @pl.when(yh < NY - 1)
            def _():
                t_all[it, lax.rem(yh + 1, NY)] = kept

        y_sends(it, lambda c: c.start())
        if it == 1:
            hear(2, lax.min(chips - 1 - chip, 1))

            @pl.when(chip < chips - 1)
            def _():
                late_copy().start()

        for j in range(NY):
            if it == 0:
                awaited = yh != j
            else:
                awaited = yh + 1 != j if j else z > 0

            @pl.when(awaited)
            def _(j=j):
                copy(t_out.at[it], t_all.at[it, j], SEM_Y, SEM_Y + NY * it + j, sibling).wait_recv()

        both = dot3(w_y, jnp.concatenate([t_all[it, j] for j in range(NY)], axis=0))
        z_out[it] = both[COARSE:]
        if it == 0:
            hear(1, NZ - 1 - z)
        for k in range(1, NZ):

            @pl.when(z + k < NZ)
            def _(k=k):
                z_copy(it, k).start()

        pre[it, other] = both[0:COARSE]
        pre_copy(it).start()

        @pl.when(z > 0)
        def _():
            for k in range(1, NZ):

                @pl.when(z >= k)
                def _(k=k):
                    z_copy(it, k).wait_recv()

            late[it, core] = dot3(w_z, jnp.concatenate([z_all[it, k] for k in range(NZ - 1)], axis=0))
            p_copy(it).start()

        copy(z_out.at[it], pre.at[it, core], SEM_PRE, SEM_PRE + it, sibling).wait_recv()
        if it == 1:

            @pl.when(chip > 0)
            def _():
                copy(z_out.at[it], f_late, SEM_LATE, SEM_LATE, sibling).wait_recv()

        @pl.when(z > 0)
        def _():
            copy(z_out.at[it], late.at[it, other], SEM_P, SEM_P + it, sibling).wait_recv()

        before = [pre[it, j] + late[it, j] for j in (0, 1)]
        stacked = jnp.concatenate(before + [f_pair[it, 0] if it == 0 else f_late[...]], axis=0)
        parts3 = dot3(w_q, stacked)
        q_out[it] = pick(parts3[COARSE : 2 * COARSE], maps[0:1])
        for k in (3, 1, 2):
            q_copy(it, k).start()
        if it == 1:

            @pl.when(tm < slices - 2)
            def _():
                copy(state, fin, SEM_END, SEM_END, at(tm + 2)).start()
        mine = pick(parts3[0:COARSE], maps[0:1])
        for k in (2, 1, 3):
            q_copy(it, k).wait_recv()
        mean = (mine + q_all[it, 0]) + (q_all[it, 1] + q_all[it, 2])
        return wide(parts3[2 * COARSE :] + pick(mean, maps[8:9]))

    def after(*steps):
        for step in steps:
            step()

    tasks = [
        functools.partial(after, report, restriction, orders),
        powers,
        z_weights,
        functools.partial(after, y_weights, q_weights),
    ]
    for n in range(PAIRS):
        ends = pair(n, tasks[n])
    correction = chain(0, ends)
    rising = stack_short(correction)
    trace = state[0:FACE, :] + dot(pro3[0:FACE, :], rising)
    send_trace(PAIRS, trace)
    state[0:FACE, :] = trace
    state[FACE:, :] = state[FACE:, :] + dot(pro3[FACE:, :], rising)

    first_to_second = copy(cand, fin, SEM_END, SEM_END, sibling)

    @pl.when(tm == 0)
    def _():
        cand[...] = state[...]
        first_to_second.start()
        for c in range(COMP):
            fin[:, c * EL : (c + 1) * EL] = node_rows(guess, c * NODES)

    for n in range(PAIRS, 2 * PAIRS):
        ends = pair(n, functools.partial(send_starts, 1) if n == PAIRS else after)
    correction = chain(1, ends)
    added = dot(pro3[...], stack_short(correction))

    @pl.when(tm > 0)
    def _():
        first_to_second.wait_recv()

    for c in range(COMP):
        for k, i in enumerate((3, 0, 1, 2)):
            rows = slice(k * FACE, (k + 1) * FACE)
            out[pl.ds(c * NODES + i, FACE, stride=4), :] = fin[rows, c * EL : (c + 1) * EL] + part(added[rows], c)

    nb_copy().wait_send()
    for n in range(2 * PAIRS):
        trace_copy(n).wait_send()
        trace2_copy(n).wait_send()
        ahead_copy(n).wait_send()
    for it in range(ITERS):

        @pl.when(tm > 0)
        def _(it=it):
            s_copy(it).wait_send()

        f_copy(it).wait_send()
        y_sends(it, lambda c: c.wait_send())
        pre_copy(it).wait_send()
        for k in (1, 2, 3):
            q_copy(it, k).wait_send()

        @pl.when(z > 0)
        def _(it=it):
            p_copy(it).wait_send()

        for k in range(1, NZ):

            @pl.when(z + k < NZ)
            def _(k=k, it=it):
                z_copy(it, k).wait_send()

    @pl.when(chip < chips - 1)
    def _():
        late_copy().wait_send()

    @pl.when(tm == 0)
    def _():
        first_to_second.wait_send()

    @pl.when(tm < slices - 2)
    def _():
        copy(state, fin, SEM_END, SEM_END + 0, sibling).wait_send()


def body(guess, deriv, viscous, jacobian, upwind, lift, restrict, prolong, coarse_self, coarse_group, neighbors, coarse_map):
    hbm = pl.BlockSpec(memory_space=pltpu.HBM)

    def buffer(*shape):
        return pltpu.VMEM(shape, f32)

    result = pl.pallas_call(
        kernel,
        out_shape=jax.ShapeDtypeStruct((COMP * NODES, EL), f32),
        in_specs=[hbm] * INPUTS,
        out_specs=pl.BlockSpec(memory_space=pltpu.VMEM),
        scratch_shapes=[
            buffer(COMP * NODES, EL),
            buffer(NODES, NODES),
            buffer(NODES, NODES),
            pltpu.SMEM((COMP, COMP), f32),
            pltpu.SMEM((COMP, COMP), f32),
            buffer(FACE, NODES),
            buffer(CNODES, NODES),
            buffer(CNODES, NODES),
            buffer(COARSE, COARSE),
            buffer(COARSE, COARSE),
            pltpu.VMEM((1, EL), jnp.int32),
            pltpu.VMEM((16, EL), jnp.int32),
            buffer(NODES, WIDE),
            buffer(NODES, WIDE),
            buffer(2 * PAIRS, FACE, WIDE),
            buffer(2 * PAIRS, FACE, WIDE),
            buffer(2 * PAIRS, FACE, WIDE),
            buffer(2 * PAIRS, FACE, WIDE),
            buffer(2 * PAIRS, FACE, WIDE),
            buffer(8, EL),
            buffer(8, EL),
            buffer(ITERS, COARSE, EL),
            buffer(ITERS, COARSE, EL),
            buffer(ITERS, COARSE, EL),
            buffer(ITERS, 2, COARSE, EL),
            buffer(COARSE, EL),
            buffer(ITERS, COARSE, EL),
            buffer(ITERS, NY, COARSE, EL),
            buffer(ITERS, COARSE, EL),
            buffer(ITERS, NZ - 1, COARSE, EL),
            buffer(ITERS, 2, COARSE, EL),
            buffer(ITERS, 2, COARSE, EL),
            buffer(ITERS, COARSE, EL),
            buffer(ITERS, 3, COARSE, EL),
            buffer(NODES, WIDE),
            buffer(NODES, WIDE),
            pltpu.VMEM((2 * NODES, 3 * NODES), bf16),
            pltpu.VMEM((NODES, 3 * FACE), bf16),
            pltpu.VMEM((CNODES, 3 * NODES), bf16),
            pltpu.VMEM((CNODES, 3 * FACE), bf16),
            pltpu.VMEM((NODES, 3 * CNODES), bf16),
            buffer(2, 4, COARSE, COARSE),
            pltpu.VMEM((2, 2 * COARSE, COARSE), bf16),
            pltpu.VMEM((2, 2 * COARSE, NY * COARSE), bf16),
            pltpu.VMEM((2, COARSE, (NZ - 1) * COARSE), bf16),
            pltpu.VMEM((2, 3 * COARSE, 3 * COARSE), bf16),
            pltpu.VMEM((16, EL), jnp.int32),
            pltpu.SemaphoreType.DMA((SEMS,)),
            pltpu.SemaphoreType.DMA((SEMS,)),
            pltpu.SemaphoreType.DMA((INPUTS,)),
            pltpu.SemaphoreType.REGULAR((4,)),
        ],
        compiler_params=pltpu.CompilerParams(
            collective_id=0, has_side_effects=True, vmem_limit_bytes=60 * 2**20
        ),
        name="parareal",
    )(
        guess.reshape(COMP * NODES, EL), deriv, viscous, jacobian, upwind, lift.T, restrict, prolong.T,
        coarse_self, coarse_group, neighbors.reshape(1, EL), coarse_map.reshape(16, EL),
    )
    return result.reshape(1, COMP, NODES, EL)


def solution(mesh):
    return jax.shard_map(
        body,
        mesh=mesh,
        in_specs=(
            P("tm", None, None, "space"),
            P(), P(), P(), P(), P(), P(), P(), P(), P(),
            P("space"),
            P(),
        ),
        out_specs=P("tm", None, None, "space"),
        check_vma=False,
    )
```

```python
import functools

import jax
import jax.numpy as jnp
from jax import lax
from jax.experimental import pallas as pl
from jax.experimental.pallas import tpu as pltpu
from jax.sharding import PartitionSpec as P

COMP = 5
NODES = 64
FACE = 16
CNODES = 8
SUB = 8
ITERS = 2
COARSE = 40
EL = 128
WIDE = COMP * EL
NY = 4
NZ = 8
STEP = 0.08

f32 = jnp.float32
bf16 = jnp.bfloat16
highest = lax.Precision.HIGHEST
MESH = pl.DeviceIdType.MESH

PAIRS = SUB // 2
TRACE = 0
TRACE2 = TRACE + PAIRS * ITERS
AHEAD = TRACE2 + PAIRS * ITERS
SEM_NB = AHEAD + PAIRS * ITERS
SEM_S = SEM_NB + 1
SEM_F = SEM_S + ITERS
SEM_LATE = SEM_F + ITERS
SEM_Y = SEM_LATE + 1
SEM_Z = SEM_Y + NY * ITERS
SEM_PRE = SEM_Z + (NZ - 1) * ITERS
SEM_P = SEM_PRE + ITERS
SEM_Q = SEM_P + ITERS
SEM_END = SEM_Q + 3 * ITERS
SEMS = SEM_END + 1
INPUTS = 12


def iota(shape, dim):
    return lax.broadcasted_iota(jnp.int32, shape, dim)


def dot(a, b):
    return jnp.dot(a, b, preferred_element_type=f32)


def dot32(a, b):
    return jnp.dot(a, b, precision=highest, preferred_element_type=f32)


def dot3(weights, x):
    high, low = halves(x)
    return dot(weights[0], high) + (dot(weights[1], high) + dot(weights[0], low))


def halves(x):
    high = x.astype(bf16)
    return high, (x - high.astype(f32)).astype(bf16)


def stack3(x):
    high, low = halves(x)
    return jnp.concatenate([high, high, low], axis=0)


def stack_short(x):
    high = x.astype(bf16).astype(f32)
    return jnp.concatenate([high, high, x - high], axis=0).astype(bf16)


def spread3(x, place):
    depth = x.shape[1]
    rows, cols = iota((depth, 3 * depth), 0), iota((depth, 3 * depth), 1)
    third = cols // depth
    hit = place(rows, cols - third * depth)
    high, low = halves(x)
    outer = jnp.where(hit & (third != 1), 1.0, 0.0).astype(bf16)
    middle = jnp.where(hit & (third == 1), 1.0, 0.0).astype(bf16)
    return (dot(high, outer) + dot(low, middle)).astype(bf16)


def same(row, col):
    return row == col


def node_place(row, col):
    return row == (col % FACE) * 4 + (col // FACE + 3) % 4


def node_rows(ref, start=0):
    return jnp.concatenate(
        [ref[pl.ds(start + i, FACE, stride=4), :] for i in (3, 0, 1, 2)], axis=0
    )


def part(x, c):
    return x[:, c * EL : (c + 1) * EL]


def pick(x, index):
    return jnp.take_along_axis(x, jnp.broadcast_to(index, x.shape), axis=1, mode="promise_in_bounds")


def tall(x):
    return jnp.concatenate([part(x, c) for c in range(COMP)], axis=0)


def wide(x):
    return jnp.concatenate([x[c * CNODES : (c + 1) * CNODES] for c in range(COMP)], axis=1)


def kernel(
    guess_in, deriv_in, viscous_in, jacobian_in, upwind_in, lift_in, restrict_in, prolong_in, self_in, group_in,
    neighbors_in, coarse_map_in,
    out,
    guess, deriv, viscous, jacobian, upwind, lift, restrict, prolong, self_ref, group_ref, neighbors, coarse_map,
    state, base, trace_out, ahead_out, trace_in, trace2_in, ahead_in, nb_out, nb_in, s_out, s_in, f_out, f_pair, f_late, t_out, t_all, z_out, z_all, pre, late, q_out, q_all, cand, fin,
    gen3, lift3, rst3, rl3, pro3, w_m, w_t, w_y, w_z, w_q, maps,
    ssem, rsem, isem, ready,
):
    loads = [
        pltpu.make_async_copy(src, dst, isem.at[k])
        for k, (src, dst) in enumerate(
            [
                (guess_in, guess),
                (viscous_in, viscous),
                (deriv_in, deriv),
                (lift_in, lift),
                (neighbors_in, neighbors),
                (jacobian_in, jacobian),
                (upwind_in, upwind),
                (restrict_in, restrict),
                (self_in, self_ref),
                (group_in, group_ref),
                (coarse_map_in, coarse_map),
                (prolong_in, prolong),
            ]
        )
    ]
    for load in loads:
        load.start()
    tm, sp = lax.axis_index("tm"), lax.axis_index("space")
    core, chip = lax.rem(tm, 2), tm // 2
    yh, z = lax.rem(chip, NY), chip // NY
    slices, parts = 2 * NY * NZ, 16

    def at(t=None, s=None):
        return {"tm": tm if t is None else t, "space": sp if s is None else s}

    other = 1 - core

    def chip_at(q, c):
        return at(2 * q + c)

    def y_at(k):
        return at((z * NY + lax.rem(yh + k + NY, NY)) * 2 + other)

    def z_at(k):
        return at(2 * (chip + NY * k) + other)

    def edge_at(target):
        return at(2 * ((z + 1) * NY + target) + other)

    def sp_at(k):
        return at(None, lax.rem(sp + k + parts, parts))

    sibling = at(tm + 1 - 2 * core)
    upper = at(lax.rem(tm + 1, slices))
    lower = at(lax.rem(tm + slices - 1, slices))

    def copy(src, dst, send, recv, to):
        return pltpu.make_async_remote_copy(
            src_ref=src, dst_ref=dst, send_sem=ssem.at[send], recv_sem=rsem.at[recv], device_id=to, device_id_type=MESH
        )

    def trace_copy(n):
        return copy(trace_out.at[n], trace_in.at[n], TRACE + n, TRACE + n, sp_at(1))

    def trace2_copy(n):
        return copy(trace_out.at[n], trace2_in.at[n], TRACE2 + n, TRACE2 + n, sp_at(2))

    def ahead_copy(n):
        return copy(ahead_out.at[n], ahead_in.at[n], AHEAD + n, AHEAD + n, sp_at(1))

    def nb_copy():
        return copy(nb_out, nb_in, SEM_NB, SEM_NB, sp_at(1))

    def send_trace(n, trace):
        trace_out[n] = trace
        trace2_copy(n).start()
        trace_copy(n).start()

    def s_copy(it):
        return copy(s_out.at[it], s_in.at[it], SEM_S + it, SEM_S + it, lower)

    def f_copy(it):
        return copy(f_out.at[it], f_pair.at[it, core], SEM_F + it, SEM_F + it, sibling)

    def late_copy():
        return copy(f_pair.at[1, 0], f_late, SEM_LATE, SEM_LATE, chip_at(chip + 1, core))

    def y_copy(it, k):
        if it == 0:
            slot, to = yh, y_at(k)
        else:
            slot = lax.rem(yh + 1, NY)
            to = at((chip // NY * NY + lax.rem(yh + k, NY) + NY * (yh // (NY - 1))) * 2 + other)
        return copy(t_out.at[it], t_all.at[it, slot], SEM_Y + NY * it + k, SEM_Y + NY * it + slot, to)

    def y_sends(it, act):
        for k in (2, 1, 3, 0):
            if it == 0:
                if k > 0:
                    act(y_copy(it, k))
            else:
                allowed = (yh == NY - 1) & (z < NZ - 1)
                if k > 0:
                    allowed = allowed | (yh < NY - 1)

                @pl.when(allowed)
                def _(k=k):
                    act(y_copy(it, k))

    def z_copy(it, k):
        sem = SEM_Z + (NZ - 1) * it + k - 1
        return copy(z_out.at[it], z_all.at[it, k - 1], sem, sem, z_at(k))

    def pre_copy(it):
        return copy(pre.at[it, other], pre.at[it, other], SEM_PRE + it, SEM_PRE + it, sibling)

    def p_copy(it):
        return copy(late.at[it, core], late.at[it, core], SEM_P + it, SEM_P + it, sibling)

    def q_copy(it, k):
        sem = SEM_Q + 3 * it + k - 1
        to = at(tm + 1 - 2 * core, lax.rem(sp + 4 * k, parts))
        return copy(q_out.at[it], q_all.at[it, k - 1], sem, sem, to)

    z_all[...] = jnp.zeros_like(z_all)
    t_all[1, 0] = jnp.zeros((COARSE, EL), f32)
    f_late[...] = jnp.zeros_like(f_late)
    late[...] = jnp.zeros_like(late)
    s_in[...] = jnp.zeros_like(s_in)

    chips = NY * NZ
    barrier = pltpu.get_barrier_semaphore()

    def tell(semaphore, device):
        pl.semaphore_signal(semaphore, inc=1, device_id=device, device_id_type=MESH)

    peers = [at(tm + 1 - 2 * core, lax.rem(sp + 4 * k, parts)) for k in (1, 2, 3)]
    for device in [sp_at(-1), sp_at(-2), sibling] + peers:
        tell(barrier, device)

    @pl.when(tm < slices - 1)
    def _():
        tell(barrier, upper)

    @pl.when(chip < chips - 1)
    def _():
        tell(barrier, chip_at(chip + 1, core))

    for k in range(1, NY):

        @pl.when(yh + k < NY)
        def _(k=k):
            tell(barrier, y_at(k))

    for k in range(1, NZ):

        @pl.when(z + k < NZ)
        def _(k=k):
            tell(barrier, z_at(k))

    last_y, first_y = yh // (NY - 1), 1 - yh // (NY - 1)

    @pl.when((yh == NY - 1) & (z < NZ - 1))
    def _():
        for target in range(NY - 1):
            tell(barrier, edge_at(target))

    heard = 6 + lax.min(tm, 1) + lax.min(chip, 1) + yh + z + first_y * lax.min(z, 1)

    def report():
        @pl.when(chip > 0)
        def _():
            tell(ready.at[2], chip_at(chip - 1, core))

        @pl.when((yh < NY - 1) & (z > 0))
        def _():
            tell(ready.at[3], at(2 * (z * NY - 1) + other))

        for k in range(1, NY):

            @pl.when(yh - k >= 0)
            def _(k=k):
                tell(ready.at[0], y_at(-k))

        for k in range(1, NZ):

            @pl.when(z - k >= 0)
            def _(k=k):
                tell(ready.at[1], z_at(-k))

    def hear(which, count):
        @pl.when(count > 0)
        def _():
            pl.semaphore_wait(ready.at[which], count)

    rows, cols = iota((NODES, NODES), 0), iota((NODES, NODES), 1)
    reorder = jnp.where(node_place(cols, rows), 1.0, 0.0)

    def reordered(flipped):
        return lax.dot_general(
            reorder, flipped, (((1,), (1,)), ((), ())), precision=highest, preferred_element_type=f32
        )

    loads[0].wait()
    for c in range(COMP):
        state[:, c * EL : (c + 1) * EL] = node_rows(guess, c * NODES)
    for load in loads[1:7]:
        load.wait()

    def sides(numbers, place):
        here = (numbers // EL) == jnp.broadcast_to(place, (1, EL))
        return numbers % EL, jnp.broadcast_to(here, (FACE, EL))

    index, own = sides(neighbors[...], sp)
    nb_out[...] = jnp.broadcast_to(neighbors[...].astype(f32), (8, EL))

    pl.semaphore_wait(barrier, heard)
    send_trace(0, state[0:FACE, :])
    nb_copy().start()

    volume = jnp.concatenate([node_rows(viscous), node_rows(deriv)], axis=0) * STEP
    gen3[...] = spread3(volume, node_place)
    lift_rows = reordered(lift[...]) * STEP
    lift3[...] = spread3(lift_rows, same)

    def volume_part(v, dest):
        yz = dot(gen3[...], stack3(v))
        for c in range(COMP):
            total = part(v, c) + part(yz[0:NODES], c)
            for d in range(COMP):
                total = total - jacobian[c, d] * part(yz[NODES:], d)
            dest[:, c * EL : (c + 1) * EL] = total

    def faces(jump):
        mixed = []
        for c in range(COMP):
            total = upwind[c, 0] * jump[0]
            for d in range(1, COMP):
                total = total + upwind[c, d] * jump[d]
            mixed.append(total)
        return stack3(jnp.concatenate(mixed, axis=1))

    def pair(n, side):
        last = n % PAIRS == PAIRS - 1
        v = state[...]
        volume_part(v, base)
        minus = [part(v[FACE : 2 * FACE], d) for d in range(COMP)]
        inner = [pick(part(v[0:FACE], d), index) for d in range(COMP)]
        known = faces([jnp.where(own, inner[d], 0.0) - minus[d] for d in range(COMP)])
        ahead_out[n] = base[0:FACE, :] + dot(lift3[0:FACE, :], known)
        ahead_copy(n).start()
        side()
        if n == 0:
            nb_copy().wait_recv()
        trace_copy(n).wait_recv()
        jump = [
            jnp.where(own, inner[d], pick(trace_in[n, :, d * EL : (d + 1) * EL], index)) - minus[d] for d in range(COMP)
        ]
        v = base[...] + dot(lift3[...], faces(jump))
        volume_part(v, base)
        if last:
            coarse_base = dot(rst3[...], stack3(base[...]))
        minus = [part(v[FACE : 2 * FACE], d) for d in range(COMP)]
        inner = [pick(part(v[0:FACE], d), index) for d in range(COMP)]
        index_before, own_before = sides(nb_in[0:1, :].astype(jnp.int32), lax.rem(sp + parts - 1, parts))
        trace2_copy(n).wait_recv()
        jump = [
            jnp.where(own_before, 0.0, pick(trace2_in[n, :, d * EL : (d + 1) * EL], index_before)) for d in range(COMP)
        ]
        missing = dot(lift3[0:FACE, :], faces(jump))
        ahead_copy(n).wait_recv()
        before = ahead_in[n] + missing
        jump = [jnp.where(own, inner[d], pick(part(before, d), index)) - minus[d] for d in range(COMP)]
        entering = faces(jump)
        if last:
            ends = coarse_base + dot(rl3[...], entering)
            return ends, entering
        trace = base[0:FACE, :] + dot(lift3[0:FACE, :], entering)
        send_trace(n + 1, trace)
        state[0:FACE, :] = trace
        state[FACE:, :] = base[FACE:, :] + dot(lift3[FACE:, :], entering)

    def send_starts(it):
        s_out[it] = tall(dot(rst3[...], stack3(state[...])))

        @pl.when(tm > 0)
        def _():
            s_copy(it).start()

    def restriction():
        for load in loads[7:]:
            load.wait()
        full = restrict[...]
        rst3[...] = spread3(full, node_place)
        pro3[...] = spread3(reordered(prolong[...]), same)
        moved = dot32(full, jnp.where(node_place(rows, cols), 1.0, 0.0))
        rl3[...] = spread3(dot32(moved, lift_rows), same)
        send_starts(0)

    def orders():
        lane = iota((16, EL), 1)
        here = pick(coarse_map[...], sp * 8 + lane % 8)
        chosen = jnp.where(iota((16, EL), 0) == lane // 8, here.astype(f32), 0.0)
        member = jnp.sum(chosen, axis=0, keepdims=True) - jnp.broadcast_to(sp * EL, (1, EL)).astype(f32)
        grid = jnp.transpose(jnp.broadcast_to(member, (EL, EL)))
        hit = grid == iota((EL, EL), 1).astype(f32)
        back = jnp.sum(jnp.where(hit, iota((EL, EL), 0).astype(f32), 0.0), axis=0, keepdims=True)
        maps[0:8] = jnp.broadcast_to(member, (8, EL)).astype(jnp.int32)
        maps[8:16] = jnp.broadcast_to(back, (8, EL)).astype(jnp.int32)

    small = (COARSE, COARSE)
    second = jnp.broadcast_to(core, small) == 1
    eye = jnp.where(iota(small, 0) == iota(small, 1), 1.0, 0.0)
    zero = jnp.zeros(small, f32)

    def put(ref, value):
        high, low = halves(value)
        ref[0] = high
        ref[1] = low

    def beside(blocks):
        return jnp.concatenate(blocks, axis=1)

    def powers():
        a = self_ref[...]
        b = a + group_ref[...]
        put(w_t, jnp.concatenate([a, b], axis=0))
        for j, m in enumerate((a, b)):
            w = dot32(m, m)
            w2 = dot32(w, w)
            w_m[j, 0] = w
            w_m[j, 1] = w2
            w_m[j, 2] = dot32(w2, w)
            w_m[j, 3] = dot32(w2, w2)

    def by_yh(choices):
        place = jnp.broadcast_to(yh, small)
        value = choices[3]
        for j in (2, 1, 0):
            value = jnp.where(place == j, choices[j], value)
        return value

    def y_weights():
        w, w2, w3 = [jnp.where(second, w_m[0, j], w_m[1, j]) for j in range(3)]
        before = beside(
            [by_yh([zero, eye, w, w2]), by_yh([zero, zero, eye, w]), by_yh([zero, zero, zero, eye]), zero]
        )
        put(w_y, jnp.concatenate([before, beside([w3, w2, w, eye])], axis=0))

    def z_weights():
        w, w2, w3, w8 = [jnp.where(second, w_m[1, j], w_m[0, j]) for j in range(4)]
        weight = by_yh([eye, w, w2, w3])
        weights = [weight]
        for k in range(NZ - 2):
            weight = dot32(weight, w8)
            weights.append(weight)
        put(w_z, beside(weights))

    def q_weights():
        a, group = self_ref[...], group_ref[...]
        b = a + group
        aa, bb = w_m[0, 0], w_m[1, 0]
        even = beside([-0.25 * a, 0.25 * b, zero])
        odd = beside([-0.25 * aa, 0.25 * bb, 0.25 * group])
        even_own, odd_own = beside([a, zero, zero]), beside([aa, zero, a])
        here = jnp.broadcast_to(core, odd.shape) == 1
        mine, sent, own = jnp.where(here, odd, even), jnp.where(here, even, odd), jnp.where(here, odd_own, even_own)
        put(w_q, jnp.concatenate([mine, sent, own], axis=0))

    def chain(it, ends, entering):
        @pl.when(tm < slices - 1)
        def _():
            s_copy(it).wait_recv()

        force = tall(ends) - s_in[it]
        f_out[it] = force
        f_copy(it).start()
        state[...] = base[...] + dot(lift3[...], entering)
        f_pair[it, core] = force
        copy(f_out.at[it], f_pair.at[it, other], SEM_F + it, SEM_F + it, sibling).wait_recv()
        both = dot3(w_t, f_pair[it, 0])
        first, other_chain = f_pair[it, 1] + both[0:COARSE], f_pair[it, 1] + both[COARSE:]
        is_second = jnp.broadcast_to(core, (COARSE, EL)) == 1
        t_out[it] = jnp.where(is_second, other_chain, first)
        kept = jnp.where(is_second, first, other_chain)
        if it == 0:
            hear(0, NY - 1 - yh)
            t_all[it, yh] = kept
        else:
            hear(3, (NY - 1) * last_y * lax.min(NZ - 1 - z, 1))

            @pl.when(yh < NY - 1)
            def _():
                t_all[it, lax.rem(yh + 1, NY)] = kept

        y_sends(it, lambda c: c.start())
        if it == 1:
            hear(2, lax.min(chips - 1 - chip, 1))

            @pl.when(chip < chips - 1)
            def _():
                late_copy().start()

        for j in range(NY):
            if it == 0:
                awaited = yh != j
            else:
                awaited = yh + 1 != j if j else z > 0

            @pl.when(awaited)
            def _(j=j):
                copy(t_out.at[it], t_all.at[it, j], SEM_Y, SEM_Y + NY * it + j, sibling).wait_recv()

        both = dot3(w_y, jnp.concatenate([t_all[it, j] for j in range(NY)], axis=0))
        z_out[it] = both[COARSE:]
        if it == 0:
            hear(1, NZ - 1 - z)
        for k in range(1, NZ):

            @pl.when(z + k < NZ)
            def _(k=k):
                z_copy(it, k).start()

        pre[it, other] = both[0:COARSE]
        pre_copy(it).start()

        @pl.when(z > 0)
        def _():
            for k in range(1, NZ):

                @pl.when(z >= k)
                def _(k=k):
                    z_copy(it, k).wait_recv()

            late[it, core] = dot3(w_z, jnp.concatenate([z_all[it, k] for k in range(NZ - 1)], axis=0))
            p_copy(it).start()

        copy(z_out.at[it], pre.at[it, core], SEM_PRE, SEM_PRE + it, sibling).wait_recv()
        if it == 1:

            @pl.when(chip > 0)
            def _():
                copy(z_out.at[it], f_late, SEM_LATE, SEM_LATE, sibling).wait_recv()

        @pl.when(z > 0)
        def _():
            copy(z_out.at[it], late.at[it, other], SEM_P, SEM_P + it, sibling).wait_recv()

        before = [pre[it, j] + late[it, j] for j in (0, 1)]
        stacked = jnp.concatenate(before + [f_pair[it, 0] if it == 0 else f_late[...]], axis=0)
        parts3 = dot3(w_q, stacked)
        q_out[it] = pick(parts3[COARSE : 2 * COARSE], maps[0:1])
        for k in (3, 1, 2):
            q_copy(it, k).start()
        if it == 1:

            @pl.when(tm < slices - 2)
            def _():
                copy(state, fin, SEM_END, SEM_END, at(tm + 2)).start()
        mine = pick(parts3[0:COARSE], maps[0:1])
        for k in (2, 1, 3):
            q_copy(it, k).wait_recv()
        mean = (mine + q_all[it, 0]) + (q_all[it, 1] + q_all[it, 2])
        return wide(parts3[2 * COARSE :] + pick(mean, maps[8:9]))

    def after(*steps):
        for step in steps:
            step()

    tasks = [
        functools.partial(after, report, restriction, orders),
        powers,
        z_weights,
        functools.partial(after, y_weights, q_weights),
    ]
    for n in range(PAIRS):
        ends = pair(n, tasks[n])
    correction = chain(0, *ends)
    rising = stack_short(correction)
    trace = state[0:FACE, :] + dot(pro3[0:FACE, :], rising)
    send_trace(PAIRS, trace)
    state[0:FACE, :] = trace
    state[FACE:, :] = state[FACE:, :] + dot(pro3[FACE:, :], rising)

    first_to_second = copy(cand, fin, SEM_END, SEM_END, sibling)

    @pl.when(tm == 0)
    def _():
        cand[...] = state[...]
        first_to_second.start()
        for c in range(COMP):
            fin[:, c * EL : (c + 1) * EL] = node_rows(guess, c * NODES)

    for n in range(PAIRS, 2 * PAIRS):
        ends = pair(n, functools.partial(send_starts, 1) if n == PAIRS else after)
    correction = chain(1, *ends)
    added = dot(pro3[...], stack_short(correction))

    @pl.when(tm > 0)
    def _():
        first_to_second.wait_recv()

    for c in range(COMP):
        for k, i in enumerate((3, 0, 1, 2)):
            rows = slice(k * FACE, (k + 1) * FACE)
            out[pl.ds(c * NODES + i, FACE, stride=4), :] = fin[rows, c * EL : (c + 1) * EL] + part(added[rows], c)

    nb_copy().wait_send()
    for n in range(2 * PAIRS):
        trace_copy(n).wait_send()
        trace2_copy(n).wait_send()
        ahead_copy(n).wait_send()
    for it in range(ITERS):

        @pl.when(tm > 0)
        def _(it=it):
            s_copy(it).wait_send()

        f_copy(it).wait_send()
        y_sends(it, lambda c: c.wait_send())
        pre_copy(it).wait_send()
        for k in (1, 2, 3):
            q_copy(it, k).wait_send()

        @pl.when(z > 0)
        def _(it=it):
            p_copy(it).wait_send()

        for k in range(1, NZ):

            @pl.when(z + k < NZ)
            def _(k=k, it=it):
                z_copy(it, k).wait_send()

    @pl.when(chip < chips - 1)
    def _():
        late_copy().wait_send()

    @pl.when(tm == 0)
    def _():
        first_to_second.wait_send()

    @pl.when(tm < slices - 2)
    def _():
        copy(state, fin, SEM_END, SEM_END + 0, sibling).wait_send()


def body(guess, deriv, viscous, jacobian, upwind, lift, restrict, prolong, coarse_self, coarse_group, neighbors, coarse_map):
    hbm = pl.BlockSpec(memory_space=pltpu.HBM)

    def buffer(*shape):
        return pltpu.VMEM(shape, f32)

    result = pl.pallas_call(
        kernel,
        out_shape=jax.ShapeDtypeStruct((COMP * NODES, EL), f32),
        in_specs=[hbm] * INPUTS,
        out_specs=pl.BlockSpec(memory_space=pltpu.VMEM),
        scratch_shapes=[
            buffer(COMP * NODES, EL),
            buffer(NODES, NODES),
            buffer(NODES, NODES),
            pltpu.SMEM((COMP, COMP), f32),
            pltpu.SMEM((COMP, COMP), f32),
            buffer(FACE, NODES),
            buffer(CNODES, NODES),
            buffer(CNODES, NODES),
            buffer(COARSE, COARSE),
            buffer(COARSE, COARSE),
            pltpu.VMEM((1, EL), jnp.int32),
            pltpu.VMEM((16, EL), jnp.int32),
            buffer(NODES, WIDE),
            buffer(NODES, WIDE),
            buffer(2 * PAIRS, FACE, WIDE),
            buffer(2 * PAIRS, FACE, WIDE),
            buffer(2 * PAIRS, FACE, WIDE),
            buffer(2 * PAIRS, FACE, WIDE),
            buffer(2 * PAIRS, FACE, WIDE),
            buffer(8, EL),
            buffer(8, EL),
            buffer(ITERS, COARSE, EL),
            buffer(ITERS, COARSE, EL),
            buffer(ITERS, COARSE, EL),
            buffer(ITERS, 2, COARSE, EL),
            buffer(COARSE, EL),
            buffer(ITERS, COARSE, EL),
            buffer(ITERS, NY, COARSE, EL),
            buffer(ITERS, COARSE, EL),
            buffer(ITERS, NZ - 1, COARSE, EL),
            buffer(ITERS, 2, COARSE, EL),
            buffer(ITERS, 2, COARSE, EL),
            buffer(ITERS, COARSE, EL),
            buffer(ITERS, 3, COARSE, EL),
            buffer(NODES, WIDE),
            buffer(NODES, WIDE),
            pltpu.VMEM((2 * NODES, 3 * NODES), bf16),
            pltpu.VMEM((NODES, 3 * FACE), bf16),
            pltpu.VMEM((CNODES, 3 * NODES), bf16),
            pltpu.VMEM((CNODES, 3 * FACE), bf16),
            pltpu.VMEM((NODES, 3 * CNODES), bf16),
            buffer(2, 4, COARSE, COARSE),
            pltpu.VMEM((2, 2 * COARSE, COARSE), bf16),
            pltpu.VMEM((2, 2 * COARSE, NY * COARSE), bf16),
            pltpu.VMEM((2, COARSE, (NZ - 1) * COARSE), bf16),
            pltpu.VMEM((2, 3 * COARSE, 3 * COARSE), bf16),
            pltpu.VMEM((16, EL), jnp.int32),
            pltpu.SemaphoreType.DMA((SEMS,)),
            pltpu.SemaphoreType.DMA((SEMS,)),
            pltpu.SemaphoreType.DMA((INPUTS,)),
            pltpu.SemaphoreType.REGULAR((4,)),
        ],
        compiler_params=pltpu.CompilerParams(
            collective_id=0, has_side_effects=True, vmem_limit_bytes=60 * 2**20
        ),
        name="parareal",
    )(
        guess.reshape(COMP * NODES, EL), deriv, viscous, jacobian, upwind, lift.T, restrict, prolong.T,
        coarse_self, coarse_group, neighbors.reshape(1, EL), coarse_map.reshape(16, EL),
    )
    return result.reshape(1, COMP, NODES, EL)


def solution(mesh):
    return jax.shard_map(
        body,
        mesh=mesh,
        in_specs=(
            P("tm", None, None, "space"),
            P(), P(), P(), P(), P(), P(), P(), P(), P(),
            P("space"),
            P(),
        ),
        out_specs=P("tm", None, None, "space"),
        check_vma=False,
    )
```
